512 devices in a mesh: fsdp: 4 (over x_hi, core), sp: 8 (over z), enc: 16 (over x_lo, y).
Axes of the slice: x: 4 (x_hi: 2, x_lo: 2; x = x_hi * 2 + x_lo), y: 8, z: 8, core: 2. Of those that a mesh axis runs over, the one named last changes fastest.
Arguments:
- image_qkv: bfloat16 [64, 1024, 3, 2048], P(('fsdp', 'enc'), 'sp'), may hold values from -6 to 6
- cotangent: bfloat16 [64, 1024, 2048], P(('fsdp', 'enc'), 'sp'), may hold values from -320 to 320
- text_kv: bfloat16 [8192, 2, 2048], P(('fsdp', 'sp', 'enc')), may hold values from -6 to 6
- routes: int32 [8192, 1], P(('fsdp', 'sp', 'enc')), may hold values from 0 to 15; in each aligned block of 16 rows (0 to 15, 16 to 31, ...) at most 2 rows name the same one
- q_gain: float32 [128], replicated, may hold values from 0.1 to 1.9
- k_gain: float32 [128], replicated, may hold values from 0.1 to 1.9
- text_gain: float32 [128], replicated, may hold values from 0.1 to 1.9
Outputs:
- image_grad: bfloat16 [64, 1024, 3, 2048], P(('fsdp', 'enc'), 'sp')
- text_grad: bfloat16 [8192, 2, 2048], P(('fsdp', 'sp', 'enc'))
- gain_grads: float32 [3, 128], replicated
The draws below stay inside these ranges and needn't reach their ends.
Inputs may be any that keep to these rules, and one draw needn't show every extreme that they name: `routes`: within the rows of one encoder shard no value appears more than 2 times, and in every draw some shard has a value exactly 2 times.
All inputs are finite; a program needn't handle non-finite values.
Results may differ from the reference program's by a relative error of at most 0.012.
The reference program's roundings to bfloat16 on the way (of `packed`, `grad_scaled` and `tangent`) count: a program that leaves them out, or rounds other values in their place, can miss the bound.
Values may be sent and summed in bfloat16 or wider, within the bound.
A program may use at most 64 MiB of HBM per device.

```python
import math
import jax
import jax.numpy as jnp
import numpy as np
from jax import lax

HD = 128
IMG_DEV = 128
TXT_DEV = 16
AW = 2048
SAMPLES = 64
S_IMG = 1024
CAP = 2
TXT_ROWS = 8192
N_SP = 8
N_ENC = 16
DEVICES = 512


def draw_cotangent(key, part):
    key = jax.random.fold_in(key, 7)
    sample_ids = jnp.arange(SAMPLES, dtype=jnp.int32)[:, None, None]
    token_ids = jnp.arange(S_IMG, dtype=jnp.int32)[None, :, None]
    device_rank = (sample_ids // N_ENC * N_SP + token_ids // IMG_DEV) * N_ENC + sample_ids % N_ENC
    position = device_rank.astype(jnp.float32) / float(max(DEVICES - 1, 1))
    noise_field = jnp.clip(jax.random.normal(key, (SAMPLES, S_IMG, AW), jnp.float32), -4.0, 4.0)
    rise_factor = jnp.exp(position * math.log(3.0))
    return (20.0 * rise_factor * noise_field).astype(jnp.bfloat16)


def block_scale(key, extent, shards, low, largest):
    factor_of = 1.0
    for axis_at, parts in shards:
        heights = jax.random.uniform(jax.random.fold_in(jax.random.fold_in(key, 6), axis_at), (parts,), jnp.float32, low / len(shards), largest / len(shards))
        factor_of = factor_of * jnp.repeat(jnp.exp(heights), extent[axis_at] // parts).reshape((-1,) + (1,) * (len(extent) - 1 - axis_at))
    return factor_of


def deal_out(key, own, number, rows, amount, top, reach, skew):
    ranking = jax.random.permutation(key, amount)
    crowded, common = portions_of(amount, rows * top, reach, skew, True), portions_of(amount, rows * top, reach, skew, False)
    places = jnp.arange(amount)

    def named(sizes, turn):
        used = int((sizes > 0).sum())
        fixed = max(1, used // 4)
        passed = fixed + (places - fixed + turn * (used - fixed)) % max(1, amount - fixed)
        return jnp.zeros((amount,), jnp.int32).at[ranking[jnp.where(places < fixed, places, passed)]].set(jnp.asarray(sizes, jnp.int32))

    sizes = jnp.where(number % 4 == 0, named(crowded, number // 4), named(common, number - number // 4 - 1))
    mixed = jax.random.permutation(jax.random.fold_in(own, 3), amount)
    donor, receiver = mixed[0:amount // 2 * 2:2], mixed[1:amount // 2 * 2:2]
    margin = jnp.minimum(sizes[donor] - 1, reach - sizes[receiver]) // 2
    margin = jnp.where((donor == ranking[0]) | (receiver == ranking[0]) | (sizes[receiver] == 0), 0, jnp.maximum(margin, 0))
    passed = jax.random.randint(jax.random.fold_in(own, 4), (amount // 2,), 0, 1 << 20) % (margin + 1)
    sizes = sizes.at[donor].add(-passed).at[receiver].add(passed)
    items = jnp.searchsorted(jnp.cumsum(sizes), jnp.arange(rows * top), side="right").astype(jnp.int32)
    table = items.reshape(top, rows).T
    table = table[jax.random.permutation(jax.random.fold_in(own, 1), rows)]
    turn = jax.random.randint(jax.random.fold_in(own, 2), (rows, 1), 0, top)
    return jnp.take_along_axis(table, (jnp.arange(top)[None, :] + turn) % top, axis=1)


def portions_of(count, total, bound, lean, full):
    loads = [(1 << 20) // math.isqrt(grade ** lean) + 1 for grade in range(1, count + 1)]
    largest = bound if full else min(bound, max(-(-total // count), total * loads[0] // sum(loads)))
    least = 1 if total - largest >= count - 1 else 0
    given, rest = [largest] + [least] * (count - 1), total - largest - least * (count - 1)
    while rest > 0:
        movable = [i for i in range(1, count) if given[i] < largest] or [i for i in range(1, count) if given[i] < bound]
        mass, left = sum([loads[i] for i in movable]), rest
        for i in movable:
            addition = min(bound - given[i], max(1, left * loads[i] // mass), rest)
            given[i] = given[i] + addition
            rest = rest - addition
    return np.array(given)


def noise(rng, shape, scale, limit, cuts=(), held_as=jnp.bfloat16):
    array = scale * jax.random.normal(rng, shape, jnp.float32)
    if cuts:
        array = array * block_scale(rng, shape, cuts, -0.22, 0.18)
    return jnp.clip(array, -limit, limit).astype(held_as)


def setup_inputs(seed: int = 0) -> dict:
    streams_of = jax.random.split(jax.random.key(seed), 8)
    image_qkv = noise(streams_of[0], (SAMPLES, S_IMG, 3, AW), 1.0, 6.0, ((0, 64), (1, 8)))
    cotangent = draw_cotangent(jax.random.fold_in(streams_of[7], 71), 0)
    text_kv = noise(streams_of[2], (TXT_ROWS, 2, AW), 1.0, 6.0, ((0, 512),))
    routes_keys = jax.random.split(jax.random.fold_in(streams_of[3], 1), TXT_ROWS // TXT_DEV)
    routes_turns = jax.random.permutation(jax.random.fold_in(streams_of[3], 3), TXT_ROWS // TXT_DEV)
    routes = jax.vmap(lambda own, number: deal_out(jax.random.fold_in(streams_of[3], 2), own, number, TXT_DEV, N_ENC, 1, CAP, 2))(routes_keys, routes_turns).reshape((TXT_ROWS, 1))
    q_gain = jnp.clip(1.0 + 0.18 * jax.random.normal(streams_of[4], (HD,), jnp.float32), 0.1, 1.9)
    k_gain = jnp.clip(1.0 + 0.18 * jax.random.normal(streams_of[5], (HD,), jnp.float32), 0.1, 1.9)
    text_gain = jnp.clip(1.0 + 0.18 * jax.random.normal(streams_of[6], (HD,), jnp.float32), 0.1, 1.9)
    return {"image_qkv": image_qkv, "cotangent": cotangent, "text_kv": text_kv, "routes": routes, "q_gain": q_gain, "k_gain": k_gain, "text_gain": text_gain}


EPSILON = 1e-06

def norm_heads(raw_rows, gain_vec):
    wide_rows = raw_rows.astype(jnp.float32)
    factor = lax.rsqrt(lax.optimization_barrier(jnp.mean(wide_rows * wide_rows, axis=-1, keepdims=True)) + EPSILON)
    unit_rows = wide_rows * factor
    return ((unit_rows * gain_vec).astype(jnp.bfloat16), unit_rows, factor)

def norm_back(grad_norm, unit_rows, factor, gain_vec):
    scaled = grad_norm * gain_vec
    inner_mean = lax.optimization_barrier(jnp.mean(scaled * unit_rows, axis=-1, keepdims=True))
    lead_axes = tuple(range(grad_norm.ndim - 1))
    return (factor * (scaled - unit_rows * inner_mean), lax.optimization_barrier(jnp.sum(grad_norm * unit_rows, axis=lead_axes)))

def reference(image_qkv, cotangent, text_kv, routes, q_gain, k_gain, text_gain):
    samples, seq_rows, _, width = image_qkv.shape
    heads = width // HD
    per_dest = 2 * TXT_DEV // N_ENC
    destination = routes[:, 0]
    shard = jnp.arange(TXT_ROWS, dtype=jnp.int32) // TXT_DEV
    dest_table = (destination.reshape(-1, TXT_DEV)[:, :, None] == jnp.arange(N_ENC, dtype=jnp.int32)[None, None, :]).astype(jnp.int32)
    rank_in_dest = lax.optimization_barrier(jnp.sum((jnp.cumsum(dest_table, axis=1) - dest_table) * dest_table, axis=2)).reshape(-1)
    fsdp_row = shard // (N_SP * N_ENC)
    sp_index = shard // N_ENC % N_SP
    enc_index = shard % N_ENC
    sample_of_row = (fsdp_row * N_ENC + destination).astype(jnp.int32)
    key_pos = ((sp_index * N_ENC + enc_index) * per_dest + rank_in_dest).astype(jnp.int32)
    text_keys = N_SP * N_ENC * per_dest
    slot_rows = jnp.zeros((samples, text_keys, 2, width), jnp.bfloat16).at[sample_of_row, key_pos].set(text_kv)
    slot_live = jnp.zeros((samples, text_keys), jnp.float32).at[sample_of_row, key_pos].set(1.0)
    score_scale = HD ** (-0.5)

    def sample_grads(sample_parts):
        qkv_rows, grad_out, text_rows, live_mask = sample_parts
        q_norm, q_unit, q_factor = norm_heads(qkv_rows[:, 0].reshape(seq_rows, heads, HD), q_gain)
        k_norm, k_unit, k_factor = norm_heads(qkv_rows[:, 1].reshape(seq_rows, heads, HD), k_gain)
        v_rows = qkv_rows[:, 2].reshape(seq_rows, heads, HD)
        t_norm, t_unit, t_factor = norm_heads(text_rows[:, 0].reshape(text_keys, heads, HD), text_gain)
        t_values = text_rows[:, 1].reshape(text_keys, heads, HD)
        key_rows = jnp.concatenate([k_norm, t_norm], axis=0).astype(jnp.float32)
        value_rows = jnp.concatenate([v_rows, t_values], axis=0).astype(jnp.float32)
        live_all = jnp.concatenate([jnp.ones((seq_rows,), jnp.float32), live_mask])
        query_wide = q_norm.astype(jnp.float32)
        scores = jnp.einsum('qhd,khd->hqk', query_wide, key_rows) * score_scale
        weight = jnp.exp(scores) * live_all[None, None, :]
        row_total = lax.optimization_barrier(jnp.sum(weight, axis=-1)).T[:, :, None]
        packed = weight.astype(jnp.bfloat16)
        packed_wide = packed.astype(jnp.float32)
        numerator = jnp.einsum('hqk,khd->qhd', packed_wide, value_rows)
        output = numerator / row_total
        grad_wide = grad_out.reshape(seq_rows, heads, HD).astype(jnp.float32)
        grad_scaled = (grad_wide / row_total).astype(jnp.bfloat16).astype(jnp.float32)
        grad_total = -lax.optimization_barrier(jnp.sum(grad_wide * output, axis=-1, keepdims=True)) / row_total
        back_prod = jnp.einsum('qhd,khd->hqk', grad_scaled, value_rows)
        grad_total_h = jnp.transpose(grad_total, (1, 0, 2))
        tangent = ((back_prod + grad_total_h) * weight * score_scale).astype(jnp.bfloat16).astype(jnp.float32)
        dq_norm = jnp.einsum('hqk,khd->qhd', tangent, key_rows)
        dk_all = jnp.einsum('hqk,qhd->khd', tangent, query_wide)
        dv_all = jnp.einsum('hqk,qhd->khd', packed_wide, grad_scaled)
        dq_rows, q_term = norm_back(dq_norm, q_unit, q_factor, q_gain)
        dk_rows, k_term = norm_back(dk_all[:seq_rows], k_unit, k_factor, k_gain)
        dt_rows, t_term = norm_back(dk_all[seq_rows:], t_unit, t_factor, text_gain)
        image_part = jnp.stack([dq_rows, dk_rows, dv_all[:seq_rows]], axis=1).reshape(seq_rows, 3, width).astype(jnp.bfloat16)
        text_part = jnp.stack([dt_rows, dv_all[seq_rows:]], axis=1).reshape(text_keys, 2, width).astype(jnp.bfloat16)
        return (image_part, text_part, jnp.stack([q_term, k_term, t_term]))
    image_grad, slot_grads, gain_terms = lax.map(sample_grads, (image_qkv, cotangent, slot_rows, slot_live))
    text_grad = slot_grads[sample_of_row, key_pos]
    scale_total = float(samples * seq_rows * heads) ** (-0.5)
    gain_grads = lax.optimization_barrier(jnp.sum(gain_terms, axis=0)) * scale_total
    return (image_grad, text_grad, gain_grads)
```

```python
import functools
import math

import jax
import jax.numpy as jnp
from jax import lax
from jax.experimental import pallas as pl
from jax.experimental.pallas import tpu as pltpu
from jax.sharding import PartitionSpec as P

EPSILON = 1e-06
CAP = 2
F32 = jnp.float32
BF16 = jnp.bfloat16
MESH = pl.DeviceIdType.MESH


def dot(a, b):
    return jnp.dot(a, b, preferred_element_type=F32)


def dot_nt(a, b):
    return lax.dot_general(a, b, (((1,), (1,)), ((), ())), preferred_element_type=F32)


def kernel(
    sizes,
    qkv,
    cot,
    txt,
    routes,
    q_gain,
    k_gain,
    t_gain,
    out_img,
    out_txt,
    out_gain,
    rows_in,
    grads_in,
    sends,
    sigma,
    sigmas,
    text_in,
    slots,
    text_keys,
    text_sends,
    slots_back,
    text_back,
    gain_own,
    gain_z,
    gain_e,
    gain_f,
    place_t,
    qn_t,
    unit_t,
    factor_t,
    g_t,
    keys,
    keys_t,
    values,
    values_t,
    weights,
    packs,
    dk_sum,
    dv_sum,
    q_term,
    kt_term,
    own_sem,
    own_head,
    own_back,
    sg_send,
    sg_recv,
    tx_send,
    tx_recv,
    fw_send,
    fw_recv,
    ct_send,
    ct_recv,
    bk_send,
    bk_recv,
    en_send,
    en_recv,
    eb_send,
    eb_recv,
    tb_send,
    tb_recv,
    gz_send,
    gz_recv,
    ge_send,
    ge_recv,
    gf_send,
    gf_recv,
):
    n_fs, n_sp, n_en = sizes
    fs, sp, en = lax.axis_index("fsdp"), lax.axis_index("sp"), lax.axis_index("enc")
    rows, width = cot.shape
    text_rows = txt.shape[1]
    hd = q_gain.shape[1]
    local = width // n_sp
    heads = local // hd
    seq = rows * n_sp
    per_enc = CAP * n_sp
    n_slots = per_enc * n_en
    n_text = text_rows * n_sp
    scale = hd ** (-0.5)
    z_steps = sorted(range(1, n_sp), key=lambda d: -min(d, n_sp - d))
    e_steps = list(range(1, n_en))
    f_steps = list(range(1, n_fs))

    def aligned(index, size):
        return pl.ds(pl.multiple_of(index * size, size), size)

    def on(axis, me, step, size):
        return {axis: lax.rem(me + step, size)}, lax.rem(me + step, size)

    barrier = pltpu.get_barrier_semaphore()
    for axis, me, steps, size in (
        ("sp", sp, z_steps, n_sp),
        ("enc", en, e_steps, n_en),
        ("fsdp", fs, f_steps, n_fs),
    ):
        for step in steps:
            pl.semaphore_signal(barrier, inc=1, device_id=on(axis, me, step, size)[0], device_id_type=MESH)

    def remote(src, dst, send, recv, device):
        return pltpu.make_async_remote_copy(
            src_ref=src, dst_ref=dst, send_sem=send, recv_sem=recv, device_id=device, device_id_type=MESH
        )

    def copy_sigma(i):
        device, _ = on("sp", sp, z_steps[i], n_sp)
        return remote(sigma, sigmas.at[aligned(sp, text_rows)], sg_send.at[i], sg_recv.at[i], device)

    def copy_text(i):
        device, peer = on("sp", sp, z_steps[i], n_sp)
        return remote(
            txt.at[:, :, aligned(peer, local)],
            text_in.at[:, aligned(sp, text_rows), :],
            tx_send.at[i],
            tx_recv.at[i],
            device,
        )

    def copy_rows(h, i):
        device, peer = on("sp", sp, z_steps[i], n_sp)
        return remote(
            qkv.at[:, :, aligned(peer * heads + h, hd)],
            rows_in.at[h, :, aligned(sp, rows), :],
            fw_send.at[h, i],
            fw_recv.at[h, i],
            device,
        )

    def copy_cot(h, i):
        device, peer = on("sp", sp, z_steps[i], n_sp)
        return remote(
            cot.at[:, aligned(peer * heads + h, hd)],
            grads_in.at[h, aligned(sp, rows), :],
            ct_send.at[h, i],
            ct_recv.at[h, i],
            device,
        )

    def copy_back(h, i):
        device, peer = on("sp", sp, z_steps[i], n_sp)
        return remote(
            sends.at[h, :, aligned(peer, rows), :],
            out_img.at[:, :, aligned(sp * heads + h, hd)],
            bk_send.at[h, i],
            bk_recv.at[h, i],
            device,
        )

    def copy_slots(i):
        device, peer = on("enc", en, e_steps[i], n_en)
        return remote(
            slots.at[aligned(peer, per_enc)],
            text_keys.at[aligned(en, per_enc)],
            en_send.at[i],
            en_recv.at[i],
            device,
        )

    def copy_slots_back(i):
        device, peer = on("enc", en, e_steps[i], n_en)
        return remote(
            text_sends.at[aligned(peer, per_enc)],
            slots_back.at[aligned(en, per_enc)],
            eb_send.at[i],
            eb_recv.at[i],
            device,
        )

    def copy_text_back(i):
        device, peer = on("sp", sp, z_steps[i], n_sp)
        return remote(
            text_back.at[:, aligned(peer, text_rows), :],
            out_txt.at[:, :, aligned(sp, local)],
            tb_send.at[i],
            tb_recv.at[i],
            device,
        )

    def copy_gain(i, level):
        axis, me, steps, size, own, dst, send, recv = (
            ("sp", sp, z_steps, n_sp, gain_own.at[0], gain_z, gz_send, gz_recv),
            ("enc", en, e_steps, n_en, gain_own.at[1], gain_e, ge_send, ge_recv),
            ("fsdp", fs, f_steps, n_fs, gain_own.at[2], gain_f, gf_send, gf_recv),
        )[level]
        device, _ = on(axis, me, steps[i], size)
        return remote(own, dst.at[me], send.at[i], recv.at[i], device)

    own_sigma = pltpu.make_async_copy(sigma, sigmas.at[aligned(sp, text_rows)], own_sem.at[0])
    own_text = pltpu.make_async_copy(
        txt.at[:, :, aligned(sp, local)], text_in.at[:, aligned(sp, text_rows), :], own_sem.at[1]
    )
    own_slots = pltpu.make_async_copy(
        slots.at[aligned(en, per_enc)], text_keys.at[aligned(en, per_enc)], own_sem.at[2]
    )
    own_slots_back = pltpu.make_async_copy(
        text_sends.at[aligned(en, per_enc)], slots_back.at[aligned(en, per_enc)], own_sem.at[3]
    )
    own_text_back = pltpu.make_async_copy(
        text_back.at[:, aligned(sp, text_rows), :], out_txt.at[:, :, aligned(sp, local)], own_sem.at[4]
    )

    def own_rows(h):
        return pltpu.make_async_copy(
            qkv.at[:, :, aligned(sp * heads + h, hd)], rows_in.at[h, :, aligned(sp, rows), :], own_head.at[0, h]
        )

    def own_cot(h):
        return pltpu.make_async_copy(
            cot.at[:, aligned(sp * heads + h, hd)], grads_in.at[h, aligned(sp, rows), :], own_head.at[1, h]
        )

    def own_image_back(h):
        return pltpu.make_async_copy(
            sends.at[h, :, aligned(sp, rows), :], out_img.at[:, :, aligned(sp * heads + h, hd)], own_back.at[h]
        )

    dest_lane = jnp.broadcast_to(routes[...].astype(F32), (text_rows, text_rows))
    row_at = lax.broadcasted_iota(jnp.int32, (text_rows, text_rows), 0)
    col_at = lax.broadcasted_iota(jnp.int32, (text_rows, text_rows), 1)
    dest_col = jnp.sum(jnp.where(row_at == col_at, dest_lane, 0.0), axis=1, keepdims=True)
    same = jnp.where((dest_col == dest_lane) & (col_at < row_at), 1.0, 0.0)
    rank = jnp.sum(same, axis=1, keepdims=True)
    shard_first = jnp.full((text_rows, 1), sp * CAP, jnp.int32).astype(F32)
    sigma[...] = jnp.broadcast_to(dest_col * per_enc + shard_first + rank, sigma.shape).astype(BF16)

    own_sigma.start()
    own_text.start()
    for h in range(heads):
        own_rows(h).start()
        own_cot(h).start()

    pl.semaphore_wait(barrier, len(z_steps) + len(e_steps) + len(f_steps))

    for i in range(len(z_steps)):
        copy_sigma(i).start()
        copy_text(i).start()
    for h in range(heads):
        for i in range(len(z_steps)):
            copy_rows(h, i).start()
            copy_cot(h, i).start()

    own_sigma.wait()
    own_text.wait()
    for i in range(len(z_steps)):
        copy_sigma(i).wait()
        copy_text(i).wait()
    slot_at = lax.broadcasted_iota(jnp.int32, (n_text, n_slots), 1).astype(F32)
    row_slot = jnp.concatenate([sigmas[...].astype(F32)] * (n_slots // sigma.shape[1]), axis=1)
    placed_t = jnp.where(row_slot == slot_at, 1.0, 0.0)
    place_t[...] = placed_t.astype(BF16)
    placed = placed_t.T
    for part in range(2):
        slots[:, part * local : (part + 1) * local] = dot(placed.astype(BF16), text_in[part]).astype(BF16)
    live_col = jnp.sum(placed, axis=1, keepdims=True)
    slots[:, 2 * local :] = jnp.broadcast_to(live_col, (n_slots, hd)).astype(BF16)
    own_slots.start()
    for i in range(len(e_steps)):
        copy_slots(i).start()
    own_slots.wait()
    for i in range(len(e_steps)):
        copy_slots(i).wait()

    chunk = 256
    q_chunk = weights.shape[1]
    n_image = seq // chunk
    key_parts = [(c * chunk, chunk, False) for c in range(n_image)] + [(seq, n_slots, True)]
    gain_col = jnp.broadcast_to(q_gain[...], (hd, hd)).T
    q_gain_t = jnp.concatenate([gain_col] * (q_chunk // hd), axis=1)

    def norm_rows(raw, gain):
        factor = lax.rsqrt(jnp.mean(raw * raw, axis=-1, keepdims=True) + EPSILON)
        unit = raw * factor
        return unit * gain, unit, factor

    def norm_rows_back(grad, unit, factor, gain):
        scaled = grad * gain
        inner = jnp.mean(scaled * unit, axis=-1, keepdims=True)
        return factor * (scaled - unit * inner)

    def one_head(h, carry):
        own_rows(h).wait()
        own_cot(h).wait()
        for i in range(len(z_steps)):
            copy_rows(h, i).wait_recv()
            copy_cot(h, i).wait_recv()

        def prepare(c, carry):
            at = aligned(c, chunk)
            raw_t = rows_in[h, 0, at, :].astype(F32).T
            factor = lax.rsqrt(jnp.mean(raw_t * raw_t, axis=0, keepdims=True) + EPSILON)
            unit = raw_t * factor
            unit_t[:, at] = unit
            factor_t[:, at] = factor
            qn_t[:, at] = (unit * q_gain_t[:, :chunk]).astype(BF16)
            g_t[:, at] = grads_in[h, at, :].astype(F32).T
            normed = norm_rows(rows_in[h, 1, at, :].astype(F32), k_gain[...])[0]
            keys[at, :] = normed.astype(BF16)
            keys_t[:, at] = normed.T.astype(BF16)
            value = rows_in[h, 2, at, :]
            values[at, :] = value
            values_t[:, at] = value.astype(F32).T.astype(BF16)
            return carry

        lax.fori_loop(0, n_image, prepare, 0)
        text_at = pl.ds(seq, n_slots)
        normed = norm_rows(text_keys[:, aligned(h, hd)].astype(F32), t_gain[...])[0]
        keys[text_at, :] = normed.astype(BF16)
        keys_t[:, text_at] = normed.T.astype(BF16)
        value = text_keys[:, aligned(heads + h, hd)]
        values[text_at, :] = value
        values_t[:, text_at] = value.astype(F32).T.astype(BF16)
        dk_sum[...] = jnp.zeros_like(dk_sum)
        dv_sum[...] = jnp.zeros_like(dv_sum)

        def queries(j, carry):
            at = aligned(j, q_chunk)
            qn = qn_t[:, at]
            total = jnp.zeros((1, q_chunk), F32)
            numer = jnp.zeros((hd, q_chunk), F32)
            for first, count, is_text in key_parts:
                part = pl.ds(first, count)
                weight = jnp.exp2(dot(keys[part, :], qn) * (scale * math.log2(math.e)))
                if is_text:
                    live = text_keys[:, 2 * local :].astype(F32)
                    weight = weight * jnp.concatenate([live] * (q_chunk // hd), axis=1)
                total += jnp.sum(weight, axis=0, keepdims=True)
                packed = weight.astype(BF16)
                weights[part, :] = weight
                packs[part, :] = packed
                numer += dot(values_t[:, part], packed)
            inverse = 1.0 / total
            scaled_wide = g_t[:, at] * inverse
            scaled = scaled_wide.astype(BF16)
            grad_total = -jnp.sum(scaled_wide * (numer * inverse), axis=0, keepdims=True)
            dq = jnp.zeros((hd, q_chunk), F32)
            for first, count, _ in key_parts:
                part = pl.ds(first, count)
                back = dot(values[part, :], scaled)
                tangent = ((back + grad_total) * weights[part, :] * scale).astype(BF16)
                dq += dot(keys_t[:, part], tangent)
                dk_sum[part, :] += dot_nt(tangent, qn)
                dv_sum[part, :] += dot_nt(packs[part, :], scaled)
            unit = unit_t[:, at]
            q_term[...] += dq * unit
            spread = dq * q_gain_t
            inner = jnp.mean(spread * unit, axis=0, keepdims=True)
            dx = factor_t[:, at] * (spread - unit * inner)
            sends[h, 0, at, :] = dx.T.astype(BF16)
            return carry

        lax.fori_loop(0, seq // q_chunk, queries, 0)

        def finish(c, carry):
            at = aligned(c, chunk)
            dk = dk_sum[at, :]
            _, unit, factor = norm_rows(rows_in[h, 1, at, :].astype(F32), k_gain[...])
            kt_term[0:1, :] += jnp.sum(dk * unit, axis=0, keepdims=True)
            sends[h, 1, at, :] = norm_rows_back(dk, unit, factor, k_gain[...]).astype(BF16)
            sends[h, 2, at, :] = dv_sum[at, :].astype(BF16)
            return carry

        lax.fori_loop(0, n_image, finish, 0)
        dk = dk_sum[text_at, :]
        _, unit, factor = norm_rows(text_keys[:, aligned(h, hd)].astype(F32), t_gain[...])
        kt_term[1:2, :] += jnp.sum(dk * unit, axis=0, keepdims=True)
        text_sends[:, aligned(h, hd)] = norm_rows_back(dk, unit, factor, t_gain[...]).astype(BF16)
        text_sends[:, aligned(heads + h, hd)] = dv_sum[text_at, :].astype(BF16)

        @pl.when(h == heads - 1)
        def _():
            gain_own[0, 0:1, :] = jnp.sum(q_term[...].T, axis=0, keepdims=True)
            gain_own[0, 1:3, :] = kt_term[0:2, :]
            gain_z[sp] = gain_own[0]
            for i in range(len(z_steps)):
                copy_gain(i, 0).start()
            own_slots_back.start()
            for i in range(len(e_steps)):
                copy_slots_back(i).start()

        for i in range(len(z_steps)):
            copy_back(h, i).start()
        own_image_back(h).start()
        return carry

    q_term[...] = jnp.zeros_like(q_term)
    kt_term[...] = jnp.zeros_like(kt_term)
    gain_own[...] = jnp.zeros_like(gain_own)
    lax.fori_loop(0, heads, one_head, 0)

    for i in range(len(z_steps)):
        copy_gain(i, 0).wait()
    gain_own[1] = jnp.sum(gain_z[...], axis=0)
    gain_e[en] = gain_own[1]
    for i in range(len(e_steps)):
        copy_gain(i, 1).start()
    own_slots_back.wait()
    for i in range(len(e_steps)):
        copy_slots_back(i).wait()
    for part in range(2):
        mine = slots_back[:, part * local : (part + 1) * local]
        text_back[part] = dot(place_t[...], mine).astype(BF16)
    own_text_back.start()
    for i in range(len(z_steps)):
        copy_text_back(i).start()
    for i in range(len(e_steps)):
        copy_gain(i, 1).wait()
    gain_own[2] = jnp.sum(gain_e[...], axis=0)
    gain_f[fs] = gain_own[2]
    for i in range(len(f_steps)):
        copy_gain(i, 2).start()
    for i in range(len(f_steps)):
        copy_gain(i, 2).wait()
    sample_count = n_fs * n_en
    scale_total = float(sample_count * seq * heads * n_sp) ** (-0.5)
    out_gain[...] = jnp.sum(gain_f[...], axis=0)[0:3, :] * scale_total

    for h in range(heads):
        for i in range(len(z_steps)):
            copy_rows(h, i).wait_send()
            copy_cot(h, i).wait_send()
            copy_back(h, i).wait()
        own_image_back(h).wait()
    own_text_back.wait()
    for i in range(len(z_steps)):
        copy_text_back(i).wait()


def on_device(sizes, image_qkv, cotangent, text_kv, routes, q_gain, k_gain, text_gain):
    n_fs, n_sp, n_en = sizes
    _, rows, _, width = image_qkv.shape
    text_rows = text_kv.shape[0]
    hd = q_gain.shape[0]
    local = width // n_sp
    heads = local // hd
    seq = rows * n_sp
    n_slots = CAP * n_sp * n_en
    n_text = text_rows * n_sp
    n_keys = seq + n_slots
    q_chunk = 256
    qkv = image_qkv[0].transpose(1, 0, 2)
    txt = text_kv.transpose(1, 0, 2)
    dma = pltpu.SemaphoreType.DMA
    z, e, f = n_sp - 1, n_en - 1, n_fs - 1
    any_spec = pl.BlockSpec(memory_space=pl.ANY)
    vmem_spec = pl.BlockSpec(memory_space=pltpu.VMEM)
    out_img, out_txt, out_gain = pl.pallas_call(
        functools.partial(kernel, sizes),
        out_shape=(
            jax.ShapeDtypeStruct((3, rows, width), BF16),
            jax.ShapeDtypeStruct((2, text_rows, width), BF16),
            jax.ShapeDtypeStruct((3, hd), F32),
        ),
        in_specs=[any_spec] * 3 + [vmem_spec] * 4,
        out_specs=(any_spec, any_spec, vmem_spec),
        scratch_shapes=[
            pltpu.VMEM((heads, 3, seq, hd), BF16),
            pltpu.VMEM((heads, seq, hd), BF16),
            pltpu.VMEM((heads, 3, seq, hd), BF16),
            pltpu.VMEM((text_rows, hd), BF16),
            pltpu.VMEM((n_text, hd), BF16),
            pltpu.VMEM((2, n_text, local), BF16),
            pltpu.VMEM((n_slots, 2 * local + hd), BF16),
            pltpu.VMEM((n_slots, 2 * local + hd), BF16),
            pltpu.VMEM((n_slots, 2 * local), BF16),
            pltpu.VMEM((n_slots, 2 * local), BF16),
            pltpu.VMEM((2, n_text, local), BF16),
            pltpu.VMEM((3, 8, hd), F32),
            pltpu.VMEM((n_sp, 8, hd), F32),
            pltpu.VMEM((n_en, 8, hd), F32),
            pltpu.VMEM((n_fs, 8, hd), F32),
            pltpu.VMEM((n_text, n_slots), BF16),
            pltpu.VMEM((hd, seq), BF16),
            pltpu.VMEM((hd, seq), F32),
            pltpu.VMEM((1, seq), F32),
            pltpu.VMEM((hd, seq), F32),
            pltpu.VMEM((n_keys, hd), BF16),
            pltpu.VMEM((hd, n_keys), BF16),
            pltpu.VMEM((n_keys, hd), BF16),
            pltpu.VMEM((hd, n_keys), BF16),
            pltpu.VMEM((n_keys, q_chunk), F32),
            pltpu.VMEM((n_keys, q_chunk), BF16),
            pltpu.VMEM((n_keys, hd), F32),
            pltpu.VMEM((n_keys, hd), F32),
            pltpu.VMEM((hd, q_chunk), F32),
            pltpu.VMEM((8, hd), F32),
            dma((5,)),
            dma((2, heads)),
            dma((heads,)),
        ]
        + [dma((z,))] * 4
        + [dma((heads, z))] * 6
        + [dma((e,))] * 4
        + [dma((z,))] * 4
        + [dma((e,))] * 2
        + [dma((f,))] * 2,
        compiler_params=pltpu.CompilerParams(
            collective_id=0, has_side_effects=True, vmem_limit_bytes=40 << 20
        ),
    )(
        qkv,
        cotangent[0],
        txt,
        routes.reshape(1, text_rows),
        q_gain.reshape(1, hd),
        k_gain.reshape(1, hd),
        text_gain.reshape(1, hd),
    )
    return out_img.transpose(1, 0, 2)[None], out_txt.transpose(1, 0, 2), out_gain


def solution(mesh):
    sizes = tuple(mesh.shape[axis] for axis in ("fsdp", "sp", "enc"))
    placed = (
        P(("fsdp", "enc"), "sp", None, None),
        P(("fsdp", "enc"), "sp", None),
        P(("fsdp", "sp", "enc"), None, None),
        P(("fsdp", "sp", "enc"), None),
        P(),
        P(),
        P(),
    )
    return jax.shard_map(
        functools.partial(on_device, sizes),
        mesh=mesh,
        in_specs=placed,
        out_specs=(P(("fsdp", "enc"), "sp", None, None), P(("fsdp", "sp", "enc"), None, None), P()),
        check_vma=False,
    )
```

```python
import functools
import math

import jax
import jax.numpy as jnp
from jax import lax
from jax.experimental import pallas as pl
from jax.experimental.pallas import tpu as pltpu
from jax.sharding import PartitionSpec as P

EPSILON = 1e-06
CAP = 2
F32 = jnp.float32
BF16 = jnp.bfloat16
MESH = pl.DeviceIdType.MESH


def dot(a, b):
    return jnp.dot(a, b, preferred_element_type=F32)


def dot_nt(a, b):
    return lax.dot_general(a, b, (((1,), (1,)), ((), ())), preferred_element_type=F32)


def kernel(
    sizes,
    qkv,
    cot,
    txt,
    routes_hbm,
    q_gain_hbm,
    k_gain_hbm,
    t_gain_hbm,
    out_img,
    out_txt,
    out_gain,
    rows_in,
    grads_in,
    sends,
    routes,
    routes_in,
    gains,
    text_in,
    slots,
    text_keys,
    text_sends,
    slots_back,
    text_back,
    gain_own,
    gain_z,
    gain_e,
    gain_f,
    place_t,
    qn_t,
    unit_t,
    factor_t,
    g_t,
    keys,
    keys_t,
    values,
    values_t,
    weights,
    packs,
    dk_sum,
    dv_sum,
    q_term,
    kt_term,
    own_sem,
    own_head,
    own_back,
    sg_send,
    sg_recv,
    tx_send,
    tx_recv,
    fw_send,
    fw_recv,
    ct_send,
    ct_recv,
    bk_send,
    bk_recv,
    en_send,
    en_recv,
    eb_send,
    eb_recv,
    tb_send,
    tb_recv,
    gz_send,
    gz_recv,
    ge_send,
    ge_recv,
    gf_send,
    gf_recv,
    above,
    line,
):
    n_fs, n_sp, n_en = sizes
    fs, sp, en = lax.axis_index("fsdp"), lax.axis_index("sp"), lax.axis_index("enc")
    rows, width = cot.shape
    text_rows = txt.shape[0]
    hd = gains.shape[2]
    q_gain, k_gain, t_gain = gains.at[0], gains.at[1], gains.at[2]
    local = width // n_sp
    heads = local // hd
    seq = rows * n_sp
    per_enc = CAP * n_sp
    n_slots = per_enc * n_en
    n_text = text_rows * n_sp
    scale = hd ** (-0.5)
    z_steps = sorted(range(1, n_sp), key=lambda d: -min(d, n_sp - d))
    e_steps = list(range(1, n_en))
    f_steps = list(range(1, n_fs))

    def aligned(index, size):
        return pl.ds(pl.multiple_of(index * size, size), size)

    def on(axis, me, step, size):
        return {axis: lax.rem(me + step, size)}, lax.rem(me + step, size)

    layer = [("enc", en, step, n_en) for step in e_steps] + [("fsdp", fs, step, n_fs) for step in f_steps]
    barrier = pltpu.get_barrier_semaphore()

    def greet(sem, axis, me, step, size):
        pl.semaphore_signal(sem, inc=1, device_id=on(axis, me, step, size)[0], device_id_type=MESH)

    for step in range(1, n_sp):

        @pl.when(sp + step < n_sp)
        def _():
            greet(barrier, "sp", sp, step, n_sp)

    @pl.when(sp == 0)
    def _():
        for peer in layer:
            greet(barrier, *peer)

    def remote(src, dst, send, recv, device):
        return pltpu.make_async_remote_copy(
            src_ref=src, dst_ref=dst, send_sem=send, recv_sem=recv, device_id=device, device_id_type=MESH
        )

    def copy_routes(i):
        device, _ = on("sp", sp, z_steps[i], n_sp)
        return remote(routes, routes_in.at[sp], sg_send.at[i], sg_recv.at[i], device)

    def copy_text(i):
        device, peer = on("sp", sp, z_steps[i], n_sp)
        return remote(
            txt.at[:, :, aligned(peer, local)],
            text_in.at[aligned(sp, text_rows)],
            tx_send.at[i],
            tx_recv.at[i],
            device,
        )

    def copy_rows(h, i):
        device, peer = on("sp", sp, z_steps[i], n_sp)
        return remote(
            qkv.at[:, :, aligned(peer * heads + h, hd)],
            rows_in.at[h, :, aligned(sp, rows), :],
            fw_send.at[h, i],
            fw_recv.at[h, i],
            device,
        )

    def copy_cot(h, i):
        device, peer = on("sp", sp, z_steps[i], n_sp)
        return remote(
            cot.at[:, aligned(peer * heads + h, hd)],
            grads_in.at[h, aligned(sp, rows), :],
            ct_send.at[h, i],
            ct_recv.at[h, i],
            device,
        )

    def copy_back(h, i):
        device, peer = on("sp", sp, z_steps[i], n_sp)
        return remote(
            sends.at[h, :, aligned(peer, rows), :],
            out_img.at[:, :, aligned(sp * heads + h, hd)],
            bk_send.at[h, i],
            bk_recv.at[h, i],
            device,
        )

    def copy_slots(i):
        device, peer = on("enc", en, e_steps[i], n_en)
        return remote(
            slots.at[aligned(peer, per_enc)],
            text_keys.at[aligned(en, per_enc)],
            en_send.at[i],
            en_recv.at[i],
            device,
        )

    def copy_slots_back(i):
        device, peer = on("enc", en, e_steps[i], n_en)
        return remote(
            text_sends.at[aligned(peer, per_enc)],
            slots_back.at[aligned(en, per_enc)],
            eb_send.at[i],
            eb_recv.at[i],
            device,
        )

    def copy_text_back(i):
        device, peer = on("sp", sp, z_steps[i], n_sp)
        return remote(
            text_back.at[aligned(peer, text_rows)],
            out_txt.at[:, :, aligned(sp, local)],
            tb_send.at[i],
            tb_recv.at[i],
            device,
        )

    def copy_gain(i, level):
        axis, me, steps, size, own, dst, send, recv = (
            ("sp", sp, z_steps, n_sp, gain_own.at[0], gain_z, gz_send, gz_recv),
            ("enc", en, e_steps, n_en, gain_own.at[1], gain_e, ge_send, ge_recv),
            ("fsdp", fs, f_steps, n_fs, gain_own.at[2], gain_f, gf_send, gf_recv),
        )[level]
        device, _ = on(axis, me, steps[i], size)
        return remote(own, dst.at[me], send.at[i], recv.at[i], device)

    fetches = [pltpu.make_async_copy(routes_hbm, routes, own_sem.at[0])] + [
        pltpu.make_async_copy(src, gains.at[n], own_sem.at[5 + n])
        for n, src in enumerate((q_gain_hbm, k_gain_hbm, t_gain_hbm))
    ]
    own_text = pltpu.make_async_copy(
        txt.at[:, :, aligned(sp, local)], text_in.at[aligned(sp, text_rows)], own_sem.at[1]
    )
    own_slots = pltpu.make_async_copy(
        slots.at[aligned(en, per_enc)], text_keys.at[aligned(en, per_enc)], own_sem.at[2]
    )
    own_slots_back = pltpu.make_async_copy(
        text_sends.at[aligned(en, per_enc)], slots_back.at[aligned(en, per_enc)], own_sem.at[3]
    )
    own_text_back = pltpu.make_async_copy(
        text_back.at[aligned(sp, text_rows)], out_txt.at[:, :, aligned(sp, local)], own_sem.at[4]
    )

    def own_rows(h):
        return pltpu.make_async_copy(
            qkv.at[:, :, aligned(sp * heads + h, hd)], rows_in.at[h, :, aligned(sp, rows), :], own_head.at[0, h]
        )

    def own_cot(h):
        return pltpu.make_async_copy(
            cot.at[:, aligned(sp * heads + h, hd)], grads_in.at[h, aligned(sp, rows), :], own_head.at[1, h]
        )

    def own_image_back(h):
        return pltpu.make_async_copy(
            sends.at[h, :, aligned(sp, rows), :], out_img.at[:, :, aligned(sp * heads + h, hd)], own_back.at[h]
        )

    for fetch in fetches:
        fetch.start()
    own_text.start()
    for h in range(heads):
        own_rows(h).start()
        own_cot(h).start()

    for fetch in fetches:
        fetch.wait()
    routes_in[sp] = routes[...]
    pl.semaphore_wait(barrier, jnp.where(sp == 0, len(layer), sp))

    def first_sends(step):
        i = z_steps.index(step)
        copy_routes(i).start()
        copy_text(i).start()
        copy_rows(0, i).start()
        copy_cot(0, i).start()

    for step in range(1, n_sp):

        @pl.when(sp + step >= n_sp)
        def _():
            greet(above.at[n_sp - step], "sp", sp, step, n_sp)

    def text_sends_to(step):
        i = z_steps.index(step)
        copy_routes(i).start()
        copy_text(i).start()

    for step in z_steps:

        @pl.when(sp + step >= n_sp)
        def _():
            text_sends_to(step)

    for step in range(1, n_sp):

        @pl.when(sp + step < n_sp)
        def _():
            pl.semaphore_wait(above.at[step], 1)
            text_sends_to(step)

    for i in range(len(z_steps)):
        copy_rows(0, i).start()
        copy_cot(0, i).start()

    for h in range(1, heads):
        for i in range(len(z_steps)):
            copy_rows(h, i).start()
            copy_cot(h, i).start()

    @pl.when(sp == 0)
    def _():
        for peer in layer:
            greet(line, *peer)
        pl.semaphore_wait(line, len(layer))
        for step in range(1, n_sp):
            greet(line, "sp", sp, step, n_sp)

    @pl.when(sp > 0)
    def _():
        pl.semaphore_wait(line, 1)

    own_text.wait()
    for i in range(len(z_steps)):
        copy_routes(i).wait()
        copy_text(i).wait()
    row_at = lax.broadcasted_iota(jnp.int32, (text_rows, text_rows), 0)
    col_at = lax.broadcasted_iota(jnp.int32, (text_rows, text_rows), 1)
    slot_at = lax.broadcasted_iota(jnp.int32, (text_rows, n_slots), 1).astype(F32)
    placed_parts = []
    for shard in range(n_sp):
        dest_lane = jnp.broadcast_to(routes_in[shard].astype(F32), (text_rows, text_rows))
        dest_col = jnp.sum(jnp.where(row_at == col_at, dest_lane, 0.0), axis=1, keepdims=True)
        same = jnp.where((dest_col == dest_lane) & (col_at < row_at), 1.0, 0.0)
        rank = jnp.sum(same, axis=1, keepdims=True)
        slot = dest_col * per_enc + (shard * CAP) + rank
        placed_parts.append(jnp.where(slot == slot_at, 1.0, 0.0))
    placed_t = jnp.concatenate(placed_parts, axis=0)
    place_t[...] = placed_t.astype(BF16)
    placed = placed_t.T
    arrived = text_in[...].astype(F32)
    for part in range(2):
        slots[:, part * local : (part + 1) * local] = dot(
            placed.astype(BF16), arrived[:, part, :].astype(BF16)
        ).astype(BF16)
    live_col = jnp.sum(placed, axis=1, keepdims=True)
    slots[:, 2 * local :] = jnp.broadcast_to(live_col, (n_slots, hd)).astype(BF16)
    own_slots.start()
    for i in range(len(e_steps)):
        copy_slots(i).start()
    own_slots.wait()
    for i in range(len(e_steps)):
        copy_slots(i).wait()

    chunk = 256
    q_chunk = weights.shape[1]
    n_image = seq // chunk
    key_parts = [(c * chunk, chunk, False) for c in range(n_image)] + [(seq, n_slots, True)]
    gain_col = jnp.broadcast_to(q_gain[...], (hd, hd)).T
    q_gain_t = jnp.concatenate([gain_col] * (q_chunk // hd), axis=1)

    def norm_rows(raw, gain):
        factor = lax.rsqrt(jnp.mean(raw * raw, axis=-1, keepdims=True) + EPSILON)
        unit = raw * factor
        return unit * gain, unit, factor

    def norm_rows_back(grad, unit, factor, gain):
        scaled = grad * gain
        inner = jnp.mean(scaled * unit, axis=-1, keepdims=True)
        return factor * (scaled - unit * inner)

    def one_head(h, carry):
        own_rows(h).wait()
        own_cot(h).wait()
        for i in range(len(z_steps)):
            copy_rows(h, i).wait_recv()
            copy_cot(h, i).wait_recv()

        def prepare(c, carry):
            at = aligned(c, chunk)
            raw_t = rows_in[h, 0, at, :].astype(F32).T
            factor = lax.rsqrt(jnp.mean(raw_t * raw_t, axis=0, keepdims=True) + EPSILON)
            unit = raw_t * factor
            unit_t[:, at] = unit
            factor_t[:, at] = factor
            qn_t[:, at] = (unit * q_gain_t[:, :chunk]).astype(BF16)
            g_t[:, at] = grads_in[h, at, :].astype(F32).T
            normed = norm_rows(rows_in[h, 1, at, :].astype(F32), k_gain[...])[0]
            keys[at, :] = normed.astype(BF16)
            keys_t[:, at] = normed.T.astype(BF16)
            value = rows_in[h, 2, at, :]
            values[at, :] = value
            values_t[:, at] = value.astype(F32).T.astype(BF16)
            return carry

        lax.fori_loop(0, n_image, prepare, 0)
        text_at = pl.ds(seq, n_slots)
        normed = norm_rows(text_keys[:, aligned(h, hd)].astype(F32), t_gain[...])[0]
        keys[text_at, :] = normed.astype(BF16)
        keys_t[:, text_at] = normed.T.astype(BF16)
        value = text_keys[:, aligned(heads + h, hd)]
        values[text_at, :] = value
        values_t[:, text_at] = value.astype(F32).T.astype(BF16)
        dk_sum[...] = jnp.zeros_like(dk_sum)
        dv_sum[...] = jnp.zeros_like(dv_sum)

        def queries(j, carry):
            at = aligned(j, q_chunk)
            qn = qn_t[:, at]
            total = jnp.zeros((1, q_chunk), F32)
            numer = jnp.zeros((hd, q_chunk), F32)
            for first, count, is_text in key_parts:
                part = pl.ds(first, count)
                weight = jnp.exp2(dot(keys[part, :], qn) * (scale * math.log2(math.e)))
                if is_text:
                    live = text_keys[:, 2 * local :].astype(F32)
                    weight = weight * jnp.concatenate([live] * (q_chunk // hd), axis=1)
                total += jnp.sum(weight, axis=0, keepdims=True)
                packed = weight.astype(BF16)
                weights[part, :] = weight
                packs[part, :] = packed
                numer += dot(values_t[:, part], packed)
            inverse = 1.0 / total
            scaled_wide = g_t[:, at] * inverse
            scaled = scaled_wide.astype(BF16)
            grad_total = -jnp.sum(scaled_wide * (numer * inverse), axis=0, keepdims=True)
            dq = jnp.zeros((hd, q_chunk), F32)
            for first, count, _ in key_parts:
                part = pl.ds(first, count)
                back = dot(values[part, :], scaled)
                tangent = ((back + grad_total) * weights[part, :] * scale).astype(BF16)
                dq += dot(keys_t[:, part], tangent)
                dk_sum[part, :] += dot_nt(tangent, qn)
                dv_sum[part, :] += dot_nt(packs[part, :], scaled)
            unit = unit_t[:, at]
            q_term[...] += dq * unit
            spread = dq * q_gain_t
            inner = jnp.mean(spread * unit, axis=0, keepdims=True)
            dx = factor_t[:, at] * (spread - unit * inner)
            sends[h, 0, at, :] = dx.T.astype(BF16)
            return carry

        lax.fori_loop(0, seq // q_chunk, queries, 0)

        def finish(c, carry):
            at = aligned(c, chunk)
            dk = dk_sum[at, :]
            _, unit, factor = norm_rows(rows_in[h, 1, at, :].astype(F32), k_gain[...])
            kt_term[0:1, :] += jnp.sum(dk * unit, axis=0, keepdims=True)
            sends[h, 1, at, :] = norm_rows_back(dk, unit, factor, k_gain[...]).astype(BF16)
            sends[h, 2, at, :] = dv_sum[at, :].astype(BF16)
            return carry

        lax.fori_loop(0, n_image, finish, 0)
        dk = dk_sum[text_at, :]
        _, unit, factor = norm_rows(text_keys[:, aligned(h, hd)].astype(F32), t_gain[...])
        kt_term[1:2, :] += jnp.sum(dk * unit, axis=0, keepdims=True)
        text_sends[:, aligned(h, hd)] = norm_rows_back(dk, unit, factor, t_gain[...]).astype(BF16)
        text_sends[:, aligned(heads + h, hd)] = dv_sum[text_at, :].astype(BF16)

        @pl.when(h == heads - 1)
        def _():
            gain_own[0, 0:1, :] = jnp.sum(q_term[...].T, axis=0, keepdims=True)
            gain_own[0, 1:3, :] = kt_term[0:2, :]
            gain_z[sp] = gain_own[0]
            for i in range(len(z_steps)):
                copy_gain(i, 0).start()
            own_slots_back.start()
            for i in range(len(e_steps)):
                copy_slots_back(i).start()

        for i in range(len(z_steps)):
            copy_back(h, i).start()
        own_image_back(h).start()
        return carry

    q_term[...] = jnp.zeros_like(q_term)
    kt_term[...] = jnp.zeros_like(kt_term)
    gain_own[...] = jnp.zeros_like(gain_own)
    lax.fori_loop(0, heads, one_head, 0)

    for i in range(len(z_steps)):
        copy_gain(i, 0).wait()
    gain_own[1] = jnp.sum(gain_z[...], axis=0)
    gain_e[en] = gain_own[1]
    for i in range(len(e_steps)):
        copy_gain(i, 1).start()
    own_slots_back.wait()
    for i in range(len(e_steps)):
        copy_slots_back(i).wait()
    mine = [dot(place_t[...], slots_back[:, part * local : (part + 1) * local]) for part in range(2)]
    text_back[...] = jnp.stack(mine, axis=1).astype(BF16)
    own_text_back.start()
    for i in range(len(z_steps)):
        copy_text_back(i).start()
    for i in range(len(e_steps)):
        copy_gain(i, 1).wait()
    gain_own[2] = jnp.sum(gain_e[...], axis=0)
    gain_f[fs] = gain_own[2]
    for i in range(len(f_steps)):
        copy_gain(i, 2).start()
    for i in range(len(f_steps)):
        copy_gain(i, 2).wait()
    sample_count = n_fs * n_en
    scale_total = float(sample_count * seq * heads * n_sp) ** (-0.5)
    out_gain[...] = jnp.sum(gain_f[...], axis=0)[0:3, :] * scale_total

    for h in range(heads):
        for i in range(len(z_steps)):
            copy_rows(h, i).wait_send()
            copy_cot(h, i).wait_send()
            copy_back(h, i).wait()
        own_image_back(h).wait()
    own_text_back.wait()
    for i in range(len(z_steps)):
        copy_text_back(i).wait()


def write_out(img, txt, gain, out_img, out_txt, out_gain, sems):
    pieces = 4
    rows = img.shape[1] // pieces
    pairs = [
        (img.at[t, p * rows : (p + 1) * rows], out_img.at[t, p * rows : (p + 1) * rows])
        for t in range(3)
        for p in range(pieces)
    ] + [(txt, out_txt), (gain, out_gain)]
    copies = [pltpu.make_async_copy(src, dst, sems.at[n]) for n, (src, dst) in enumerate(pairs)]
    for copy in copies:
        copy.start()
    for copy in copies:
        copy.wait()


def on_device(sizes, image_qkv, cotangent, text_kv, routes, q_gain, k_gain, text_gain):
    n_fs, n_sp, n_en = sizes
    _, rows, _, width = image_qkv.shape
    text_rows = text_kv.shape[0]
    hd = q_gain.shape[0]
    local = width // n_sp
    heads = local // hd
    seq = rows * n_sp
    n_slots = CAP * n_sp * n_en
    n_text = text_rows * n_sp
    n_keys = seq + n_slots
    q_chunk = 256
    qkv = image_qkv[0].transpose(1, 0, 2)
    dma = pltpu.SemaphoreType.DMA
    z, e, f = n_sp - 1, n_en - 1, n_fs - 1
    any_spec = pl.BlockSpec(memory_space=pl.ANY)
    hbm_spec = pl.BlockSpec(memory_space=pltpu.HBM)
    vmem_spec = pl.BlockSpec(memory_space=pltpu.VMEM)
    out_img, out_txt, out_gain = pl.pallas_call(
        functools.partial(kernel, sizes),
        out_shape=(
            pltpu.VMEM((3, rows, width), BF16),
            pltpu.VMEM((text_rows, 2, width), BF16),
            pltpu.VMEM((3, hd), F32),
        ),
        in_specs=[hbm_spec] * 7,
        out_specs=(any_spec, any_spec, vmem_spec),
        scratch_shapes=[
            pltpu.VMEM((heads, 3, seq, hd), BF16),
            pltpu.VMEM((heads, seq, hd), BF16),
            pltpu.VMEM((heads, 3, seq, hd), BF16),
            pltpu.VMEM((1, text_rows), jnp.int32),
            pltpu.VMEM((n_sp, 1, text_rows), jnp.int32),
            pltpu.VMEM((3, 1, hd), F32),
            pltpu.VMEM((n_text, 2, local), BF16),
            pltpu.VMEM((n_slots, 2 * local + hd), BF16),
            pltpu.VMEM((n_slots, 2 * local + hd), BF16),
            pltpu.VMEM((n_slots, 2 * local), BF16),
            pltpu.VMEM((n_slots, 2 * local), BF16),
            pltpu.VMEM((n_text, 2, local), BF16),
            pltpu.VMEM((3, 8, hd), F32),
            pltpu.VMEM((n_sp, 8, hd), F32),
            pltpu.VMEM((n_en, 8, hd), F32),
            pltpu.VMEM((n_fs, 8, hd), F32),
            pltpu.VMEM((n_text, n_slots), BF16),
            pltpu.VMEM((hd, seq), BF16),
            pltpu.VMEM((hd, seq), F32),
            pltpu.VMEM((1, seq), F32),
            pltpu.VMEM((hd, seq), F32),
            pltpu.VMEM((n_keys, hd), BF16),
            pltpu.VMEM((hd, n_keys), BF16),
            pltpu.VMEM((n_keys, hd), BF16),
            pltpu.VMEM((hd, n_keys), BF16),
            pltpu.VMEM((n_keys, q_chunk), F32),
            pltpu.VMEM((n_keys, q_chunk), BF16),
            pltpu.VMEM((n_keys, hd), F32),
            pltpu.VMEM((n_keys, hd), F32),
            pltpu.VMEM((hd, q_chunk), F32),
            pltpu.VMEM((8, hd), F32),
            dma((8,)),
            dma((2, heads)),
            dma((heads,)),
        ]
        + [dma((z,))] * 4
        + [dma((heads, z))] * 6
        + [dma((e,))] * 4
        + [dma((z,))] * 4
        + [dma((e,))] * 2
        + [dma((f,))] * 2
        + [pltpu.SemaphoreType.REGULAR((n_sp,)), pltpu.SemaphoreType.REGULAR],
        compiler_params=pltpu.CompilerParams(
            collective_id=0, has_side_effects=True, vmem_limit_bytes=40 << 20
        ),
    )(
        *(
            pltpu.with_memory_space_constraint(operand, pltpu.HBM)
            for operand in (
                qkv,
                cotangent[0],
                text_kv,
                routes.reshape(1, text_rows),
                q_gain.reshape(1, hd),
                k_gain.reshape(1, hd),
                text_gain.reshape(1, hd),
            )
        )
    )
    results = (out_img, out_txt, out_gain)
    out_img, out_txt, out_gain = pl.pallas_call(
        write_out,
        out_shape=tuple(jax.ShapeDtypeStruct(r.shape, r.dtype) for r in results),
        in_specs=[vmem_spec] * 3,
        out_specs=(hbm_spec,) * 3,
        scratch_shapes=[dma((14,))],
    )(*(pltpu.with_memory_space_constraint(result, pltpu.VMEM) for result in results))
    return out_img.transpose(1, 0, 2)[None], out_txt, out_gain


def solution(mesh):
    sizes = tuple(mesh.shape[axis] for axis in ("fsdp", "sp", "enc"))
    placed = (
        P(("fsdp", "enc"), "sp", None, None),
        P(("fsdp", "enc"), "sp", None),
        P(("fsdp", "sp", "enc"), None, None),
        P(("fsdp", "sp", "enc"), None),
        P(),
        P(),
        P(),
    )
    return jax.shard_map(
        functools.partial(on_device, sizes),
        mesh=mesh,
        in_specs=placed,
        out_specs=(P(("fsdp", "enc"), "sp", None, None), P(("fsdp", "sp", "enc"), None, None), P()),
        check_vma=False,
    )
```

```python
import functools
import math

import jax
import jax.numpy as jnp
from jax import lax
from jax.experimental import pallas as pl
from jax.experimental.pallas import tpu as pltpu
from jax.sharding import PartitionSpec as P

EPSILON = 1e-06
CAP = 2
F32 = jnp.float32
BF16 = jnp.bfloat16
MESH = pl.DeviceIdType.MESH


def dot(a, b):
    return jnp.dot(a, b, preferred_element_type=F32)


def dot_nt(a, b):
    return lax.dot_general(a, b, (((1,), (1,)), ((), ())), preferred_element_type=F32)


def kernel(
    sizes,
    qkv,
    cot,
    txt,
    routes_hbm,
    q_gain_hbm,
    k_gain_hbm,
    t_gain_hbm,
    out_img,
    out_txt,
    out_gain,
    rows_in,
    grads_in,
    sends,
    routes_in,
    gains,
    text_in,
    slots,
    text_keys,
    text_sends,
    slots_back,
    text_back,
    gain_own,
    gain_z,
    gain_e,
    gain_f,
    place_t,
    qn_t,
    unit_t,
    factor_t,
    g_t,
    keys,
    keys_t,
    values,
    values_t,
    weights,
    packs,
    dk_sum,
    dv_sum,
    q_term,
    kt_term,
    own_sem,
    own_head,
    own_back,
    sg_send,
    sg_recv,
    tx_send,
    tx_recv,
    fw_send,
    fw_recv,
    ct_send,
    ct_recv,
    bk_send,
    bk_recv,
    en_send,
    en_recv,
    eb_send,
    eb_recv,
    tb_send,
    tb_recv,
    gz_send,
    gz_recv,
    ge_send,
    ge_recv,
    gf_send,
    gf_recv,
    above,
    line,
):
    n_fs, n_sp, n_en = sizes
    fs, sp, en = lax.axis_index("fsdp"), lax.axis_index("sp"), lax.axis_index("enc")
    rows, width = cot.shape
    text_rows = txt.shape[0]
    hd = gains.shape[2]
    q_gain, k_gain, t_gain = gains.at[0], gains.at[1], gains.at[2]
    local = width // n_sp
    heads = local // hd
    seq = rows * n_sp
    per_enc = CAP * n_sp
    n_slots = per_enc * n_en
    n_text = text_rows * n_sp
    scale = hd ** (-0.5)
    z_steps = sorted(range(1, n_sp), key=lambda d: min(d, n_sp - d))
    e_steps = list(range(1, n_en))
    f_steps = list(range(1, n_fs))

    def aligned(index, size):
        return pl.ds(pl.multiple_of(index * size, size), size)

    def on(axis, me, step, size):
        return {axis: lax.rem(me + step, size)}, lax.rem(me + step, size)

    layer = [("enc", en, step, n_en) for step in e_steps] + [("fsdp", fs, step, n_fs) for step in f_steps]
    barrier = pltpu.get_barrier_semaphore()

    def greet(sem, axis, me, step, size):
        pl.semaphore_signal(sem, inc=1, device_id=on(axis, me, step, size)[0], device_id_type=MESH)

    for step in range(1, n_sp):

        @pl.when(sp + step < n_sp)
        def _():
            greet(barrier, "sp", sp, step, n_sp)

    @pl.when(sp == 0)
    def _():
        for peer in layer:
            greet(barrier, *peer)

    def remote(src, dst, send, recv, device):
        return pltpu.make_async_remote_copy(
            src_ref=src, dst_ref=dst, send_sem=send, recv_sem=recv, device_id=device, device_id_type=MESH
        )

    def copy_routes(i):
        device, _ = on("sp", sp, z_steps[i], n_sp)
        return remote(routes_hbm, routes_in.at[sp], sg_send.at[i], sg_recv.at[i], device)

    def copy_text(i):
        device, peer = on("sp", sp, z_steps[i], n_sp)
        return remote(
            txt.at[:, :, aligned(peer, local)],
            text_in.at[aligned(sp, text_rows)],
            tx_send.at[i],
            tx_recv.at[i],
            device,
        )

    def copy_rows(h, i):
        device, peer = on("sp", sp, z_steps[i], n_sp)
        return remote(
            qkv.at[:, :, aligned(peer * heads + h, hd)],
            rows_in.at[h, :, aligned(sp, rows), :],
            fw_send.at[h, i],
            fw_recv.at[h, i],
            device,
        )

    def copy_cot(h, i):
        device, peer = on("sp", sp, z_steps[i], n_sp)
        return remote(
            cot.at[:, aligned(peer * heads + h, hd)],
            grads_in.at[h, aligned(sp, rows), :],
            ct_send.at[h, i],
            ct_recv.at[h, i],
            device,
        )

    def copy_back(h, i):
        device, peer = on("sp", sp, z_steps[i], n_sp)
        return remote(
            sends.at[h, :, aligned(peer, rows), :],
            out_img.at[:, :, aligned(sp * heads + h, hd)],
            bk_send.at[h, i],
            bk_recv.at[h, i],
            device,
        )

    def copy_slots(i):
        device, peer = on("enc", en, e_steps[i], n_en)
        return remote(
            slots.at[aligned(peer, per_enc)],
            text_keys.at[aligned(en, per_enc)],
            en_send.at[i],
            en_recv.at[i],
            device,
        )

    def copy_slots_back(i):
        device, peer = on("enc", en, e_steps[i], n_en)
        return remote(
            text_sends.at[aligned(peer, per_enc)],
            slots_back.at[aligned(en, per_enc)],
            eb_send.at[i],
            eb_recv.at[i],
            device,
        )

    def copy_text_back(i):
        device, peer = on("sp", sp, z_steps[i], n_sp)
        return remote(
            text_back.at[aligned(peer, text_rows)],
            out_txt.at[:, :, aligned(sp, local)],
            tb_send.at[i],
            tb_recv.at[i],
            device,
        )

    def copy_gain(i, level):
        axis, me, steps, size, own, dst, send, recv = (
            ("sp", sp, z_steps, n_sp, gain_own.at[0], gain_z, gz_send, gz_recv),
            ("enc", en, e_steps, n_en, gain_own.at[1], gain_e, ge_send, ge_recv),
            ("fsdp", fs, f_steps, n_fs, gain_own.at[2], gain_f, gf_send, gf_recv),
        )[level]
        device, _ = on(axis, me, steps[i], size)
        return remote(own, dst.at[me], send.at[i], recv.at[i], device)

    fetches = [pltpu.make_async_copy(routes_hbm, routes_in.at[sp], own_sem.at[0])] + [
        pltpu.make_async_copy(src, gains.at[n], own_sem.at[5 + n])
        for n, src in enumerate((q_gain_hbm, k_gain_hbm, t_gain_hbm))
    ]
    own_text = pltpu.make_async_copy(
        txt.at[:, :, aligned(sp, local)], text_in.at[aligned(sp, text_rows)], own_sem.at[1]
    )
    own_slots = pltpu.make_async_copy(
        slots.at[aligned(en, per_enc)], text_keys.at[aligned(en, per_enc)], own_sem.at[2]
    )
    own_slots_back = pltpu.make_async_copy(
        text_sends.at[aligned(en, per_enc)], slots_back.at[aligned(en, per_enc)], own_sem.at[3]
    )
    own_text_back = pltpu.make_async_copy(
        text_back.at[aligned(sp, text_rows)], out_txt.at[:, :, aligned(sp, local)], own_sem.at[4]
    )

    def own_rows(h):
        return pltpu.make_async_copy(
            qkv.at[:, :, aligned(sp * heads + h, hd)], rows_in.at[h, :, aligned(sp, rows), :], own_head.at[0, h]
        )

    def own_cot(h):
        return pltpu.make_async_copy(
            cot.at[:, aligned(sp * heads + h, hd)], grads_in.at[h, aligned(sp, rows), :], own_head.at[1, h]
        )

    def own_image_back(h):
        return pltpu.make_async_copy(
            sends.at[h, :, aligned(sp, rows), :], out_img.at[:, :, aligned(sp * heads + h, hd)], own_back.at[h]
        )

    pl.semaphore_wait(barrier, jnp.where(sp == 0, len(layer), sp))

    for step in range(1, n_sp):

        @pl.when(sp + step >= n_sp)
        def _():
            greet(above.at[n_sp - step], "sp", sp, step, n_sp)

    for fetch in fetches:
        fetch.start()
    own_text.start()
    for h in range(heads):
        own_rows(h).start()
        own_cot(h).start()

    def text_sends_to(step):
        i = z_steps.index(step)
        copy_routes(i).start()
        copy_text(i).start()

    def head_sends_to(step):
        i = z_steps.index(step)
        copy_rows(0, i).start()
        copy_cot(0, i).start()

    for step in z_steps:

        @pl.when(sp + step >= n_sp)
        def _():
            text_sends_to(step)

    for step in range(1, n_sp - 1):

        @pl.when(sp + step < n_sp - 1)
        def _():
            pl.semaphore_wait(above.at[step], 1)
            text_sends_to(step)

    for step in z_steps:

        @pl.when(sp + step != n_sp - 1)
        def _():
            head_sends_to(step)

    for step in range(1, n_sp):

        @pl.when(sp + step == n_sp - 1)
        def _():
            pl.semaphore_wait(above.at[step], 1)
            text_sends_to(step)
            head_sends_to(step)


    for h in range(1, heads):
        for i in range(len(z_steps)):
            copy_rows(h, i).start()
            copy_cot(h, i).start()

    @pl.when(sp == 0)
    def _():
        for peer in layer:
            greet(line, *peer)
        pl.semaphore_wait(line, len(layer))
        for step in range(1, n_sp):
            greet(line, "sp", sp, step, n_sp)

    @pl.when(sp > 0)
    def _():
        pl.semaphore_wait(line, 1)

    own_text.wait()
    for fetch in fetches:
        fetch.wait()
    for i in range(len(z_steps)):
        copy_routes(i).wait()
        copy_text(i).wait()
    row_at = lax.broadcasted_iota(jnp.int32, (text_rows, text_rows), 0)
    col_at = lax.broadcasted_iota(jnp.int32, (text_rows, text_rows), 1)
    slot_at = lax.broadcasted_iota(jnp.int32, (text_rows, n_slots), 1).astype(F32)
    placed_parts = []
    for shard in range(n_sp):
        dest_lane = jnp.broadcast_to(routes_in[shard].astype(F32), (text_rows, text_rows))
        dest_col = jnp.sum(jnp.where(row_at == col_at, dest_lane, 0.0), axis=1, keepdims=True)
        same = jnp.where((dest_col == dest_lane) & (col_at < row_at), 1.0, 0.0)
        rank = jnp.sum(same, axis=1, keepdims=True)
        slot = dest_col * per_enc + (shard * CAP) + rank
        placed_parts.append(jnp.where(slot == slot_at, 1.0, 0.0))
    placed_t = jnp.concatenate(placed_parts, axis=0)
    place_t[...] = placed_t.astype(BF16)
    placed = placed_t.T
    arrived = text_in[...].astype(F32)
    for part in range(2):
        slots[:, part * local : (part + 1) * local] = dot(
            placed.astype(BF16), arrived[:, part, :].astype(BF16)
        ).astype(BF16)
    live_col = jnp.sum(placed, axis=1, keepdims=True)
    slots[:, 2 * local :] = jnp.broadcast_to(live_col, (n_slots, hd)).astype(BF16)
    own_slots.start()
    for i in range(len(e_steps)):
        copy_slots(i).start()
    own_slots.wait()
    for i in range(len(e_steps)):
        copy_slots(i).wait()

    chunk = 256
    q_chunk = weights.shape[1]
    n_image = seq // chunk
    key_parts = [(c * chunk, chunk, False) for c in range(n_image)] + [(seq, n_slots, True)]
    gain_col = jnp.broadcast_to(q_gain[...], (hd, hd)).T
    q_gain_t = jnp.concatenate([gain_col] * (q_chunk // hd), axis=1)

    def norm_rows(raw, gain):
        factor = lax.rsqrt(jnp.mean(raw * raw, axis=-1, keepdims=True) + EPSILON)
        unit = raw * factor
        return unit * gain, unit, factor

    def norm_rows_back(grad, unit, factor, gain):
        scaled = grad * gain
        inner = jnp.mean(scaled * unit, axis=-1, keepdims=True)
        return factor * (scaled - unit * inner)

    def one_head(h, carry):
        own_rows(h).wait()
        own_cot(h).wait()
        for i in range(len(z_steps)):
            copy_rows(h, i).wait_recv()
            copy_cot(h, i).wait_recv()

        def prepare(c, carry):
            at = aligned(c, chunk)
            raw_t = rows_in[h, 0, at, :].astype(F32).T
            factor = lax.rsqrt(jnp.mean(raw_t * raw_t, axis=0, keepdims=True) + EPSILON)
            unit = raw_t * factor
            unit_t[:, at] = unit
            factor_t[:, at] = factor
            qn_t[:, at] = (unit * q_gain_t[:, :chunk]).astype(BF16)
            g_t[:, at] = grads_in[h, at, :].astype(F32).T
            normed = norm_rows(rows_in[h, 1, at, :].astype(F32), k_gain[...])[0]
            keys[at, :] = normed.astype(BF16)
            keys_t[:, at] = normed.T.astype(BF16)
            value = rows_in[h, 2, at, :]
            values[at, :] = value
            values_t[:, at] = value.astype(F32).T.astype(BF16)
            return carry

        lax.fori_loop(0, n_image, prepare, 0)
        text_at = pl.ds(seq, n_slots)
        normed = norm_rows(text_keys[:, aligned(h, hd)].astype(F32), t_gain[...])[0]
        keys[text_at, :] = normed.astype(BF16)
        keys_t[:, text_at] = normed.T.astype(BF16)
        value = text_keys[:, aligned(heads + h, hd)]
        values[text_at, :] = value
        values_t[:, text_at] = value.astype(F32).T.astype(BF16)
        dk_sum[...] = jnp.zeros_like(dk_sum)
        dv_sum[...] = jnp.zeros_like(dv_sum)

        def queries(j, carry):
            at = aligned(j, q_chunk)
            qn = qn_t[:, at]
            total = jnp.zeros((1, q_chunk), F32)
            numer = jnp.zeros((hd, q_chunk), F32)
            for first, count, is_text in key_parts:
                part = pl.ds(first, count)
                weight = jnp.exp2(dot(keys[part, :], qn) * (scale * math.log2(math.e)))
                if is_text:
                    live = text_keys[:, 2 * local :].astype(F32)
                    weight = weight * jnp.concatenate([live] * (q_chunk // hd), axis=1)
                total += jnp.sum(weight, axis=0, keepdims=True)
                packed = weight.astype(BF16)
                weights[part, :] = weight
                packs[part, :] = packed
                numer += dot(values_t[:, part], packed)
            inverse = 1.0 / total
            scaled_wide = g_t[:, at] * inverse
            scaled = scaled_wide.astype(BF16)
            grad_total = -jnp.sum(scaled_wide * (numer * inverse), axis=0, keepdims=True)
            dq = jnp.zeros((hd, q_chunk), F32)
            for first, count, _ in key_parts:
                part = pl.ds(first, count)
                back = dot(values[part, :], scaled)
                tangent = ((back + grad_total) * weights[part, :] * scale).astype(BF16)
                dq += dot(keys_t[:, part], tangent)
                dk_sum[part, :] += dot_nt(tangent, qn)
                dv_sum[part, :] += dot_nt(packs[part, :], scaled)
            unit = unit_t[:, at]
            q_term[...] += dq * unit
            spread = dq * q_gain_t
            inner = jnp.mean(spread * unit, axis=0, keepdims=True)
            dx = factor_t[:, at] * (spread - unit * inner)
            sends[h, 0, at, :] = dx.T.astype(BF16)
            return carry

        lax.fori_loop(0, seq // q_chunk, queries, 0)

        def finish(c, carry):
            at = aligned(c, chunk)
            dk = dk_sum[at, :]
            _, unit, factor = norm_rows(rows_in[h, 1, at, :].astype(F32), k_gain[...])
            kt_term[0:1, :] += jnp.sum(dk * unit, axis=0, keepdims=True)
            sends[h, 1, at, :] = norm_rows_back(dk, unit, factor, k_gain[...]).astype(BF16)
            sends[h, 2, at, :] = dv_sum[at, :].astype(BF16)
            return carry

        lax.fori_loop(0, n_image, finish, 0)
        dk = dk_sum[text_at, :]
        _, unit, factor = norm_rows(text_keys[:, aligned(h, hd)].astype(F32), t_gain[...])
        kt_term[1:2, :] += jnp.sum(dk * unit, axis=0, keepdims=True)
        text_sends[:, aligned(h, hd)] = norm_rows_back(dk, unit, factor, t_gain[...]).astype(BF16)
        text_sends[:, aligned(heads + h, hd)] = dv_sum[text_at, :].astype(BF16)

        @pl.when(h == heads - 1)
        def _():
            gain_own[0, 0:1, :] = jnp.sum(q_term[...].T, axis=0, keepdims=True)
            gain_own[0, 1:3, :] = kt_term[0:2, :]
            gain_z[sp] = gain_own[0]
            for i in range(len(z_steps)):
                copy_gain(i, 0).start()
            own_slots_back.start()
            for i in range(len(e_steps)):
                copy_slots_back(i).start()

        for i in range(len(z_steps)):
            copy_back(h, i).start()
        own_image_back(h).start()
        return carry

    q_term[...] = jnp.zeros_like(q_term)
    kt_term[...] = jnp.zeros_like(kt_term)
    gain_own[...] = jnp.zeros_like(gain_own)
    lax.fori_loop(0, heads, one_head, 0)

    for i in range(len(z_steps)):
        copy_gain(i, 0).wait()
    gain_own[1] = jnp.sum(gain_z[...], axis=0)
    gain_e[en] = gain_own[1]
    for i in range(len(e_steps)):
        copy_gain(i, 1).start()
    own_slots_back.wait()
    for i in range(len(e_steps)):
        copy_slots_back(i).wait()
    mine = [dot(place_t[...], slots_back[:, part * local : (part + 1) * local]) for part in range(2)]
    text_back[...] = jnp.stack(mine, axis=1).astype(BF16)
    own_text_back.start()
    for i in range(len(z_steps)):
        copy_text_back(i).start()
    for i in range(len(e_steps)):
        copy_gain(i, 1).wait()
    gain_own[2] = jnp.sum(gain_e[...], axis=0)
    gain_f[fs] = gain_own[2]
    for i in range(len(f_steps)):
        copy_gain(i, 2).start()
    for i in range(len(f_steps)):
        copy_gain(i, 2).wait()
    sample_count = n_fs * n_en
    scale_total = float(sample_count * seq * heads * n_sp) ** (-0.5)
    out_gain[...] = jnp.sum(gain_f[...], axis=0)[0:3, :] * scale_total

    for h in range(heads):
        for i in range(len(z_steps)):
            copy_rows(h, i).wait_send()
            copy_cot(h, i).wait_send()
            copy_back(h, i).wait()
        own_image_back(h).wait()
    own_text_back.wait()
    for i in range(len(z_steps)):
        copy_text_back(i).wait()


def write_out(img, txt, gain, out_img, out_txt, out_gain, sems):
    pieces = 4
    rows = img.shape[1] // pieces
    pairs = [
        (img.at[t, p * rows : (p + 1) * rows], out_img.at[t, p * rows : (p + 1) * rows])
        for t in range(3)
        for p in range(pieces)
    ] + [(txt, out_txt), (gain, out_gain)]
    copies = [pltpu.make_async_copy(src, dst, sems.at[n]) for n, (src, dst) in enumerate(pairs)]
    for copy in copies:
        copy.start()
    for copy in copies:
        copy.wait()


def on_device(sizes, image_qkv, cotangent, text_kv, routes, q_gain, k_gain, text_gain):
    n_fs, n_sp, n_en = sizes
    _, rows, _, width = image_qkv.shape
    text_rows = text_kv.shape[0]
    hd = q_gain.shape[0]
    local = width // n_sp
    heads = local // hd
    seq = rows * n_sp
    n_slots = CAP * n_sp * n_en
    n_text = text_rows * n_sp
    n_keys = seq + n_slots
    q_chunk = 256
    qkv = image_qkv[0].transpose(1, 0, 2)
    dma = pltpu.SemaphoreType.DMA
    z, e, f = n_sp - 1, n_en - 1, n_fs - 1
    any_spec = pl.BlockSpec(memory_space=pl.ANY)
    hbm_spec = pl.BlockSpec(memory_space=pltpu.HBM)
    vmem_spec = pl.BlockSpec(memory_space=pltpu.VMEM)
    out_img, out_txt, out_gain = pl.pallas_call(
        functools.partial(kernel, sizes),
        out_shape=(
            pltpu.VMEM((3, rows, width), BF16),
            pltpu.VMEM((text_rows, 2, width), BF16),
            pltpu.VMEM((3, hd), F32),
        ),
        in_specs=[hbm_spec] * 7,
        out_specs=(any_spec, any_spec, vmem_spec),
        scratch_shapes=[
            pltpu.VMEM((heads, 3, seq, hd), BF16),
            pltpu.VMEM((heads, seq, hd), BF16),
            pltpu.VMEM((heads, 3, seq, hd), BF16),
            pltpu.VMEM((n_sp, 1, text_rows), jnp.int32),
            pltpu.VMEM((3, 1, hd), F32),
            pltpu.VMEM((n_text, 2, local), BF16),
            pltpu.VMEM((n_slots, 2 * local + hd), BF16),
            pltpu.VMEM((n_slots, 2 * local + hd), BF16),
            pltpu.VMEM((n_slots, 2 * local), BF16),
            pltpu.VMEM((n_slots, 2 * local), BF16),
            pltpu.VMEM((n_text, 2, local), BF16),
            pltpu.VMEM((3, 8, hd), F32),
            pltpu.VMEM((n_sp, 8, hd), F32),
            pltpu.VMEM((n_en, 8, hd), F32),
            pltpu.VMEM((n_fs, 8, hd), F32),
            pltpu.VMEM((n_text, n_slots), BF16),
            pltpu.VMEM((hd, seq), BF16),
            pltpu.VMEM((hd, seq), F32),
            pltpu.VMEM((1, seq), F32),
            pltpu.VMEM((hd, seq), F32),
            pltpu.VMEM((n_keys, hd), BF16),
            pltpu.VMEM((hd, n_keys), BF16),
            pltpu.VMEM((n_keys, hd), BF16),
            pltpu.VMEM((hd, n_keys), BF16),
            pltpu.VMEM((n_keys, q_chunk), F32),
            pltpu.VMEM((n_keys, q_chunk), BF16),
            pltpu.VMEM((n_keys, hd), F32),
            pltpu.VMEM((n_keys, hd), F32),
            pltpu.VMEM((hd, q_chunk), F32),
            pltpu.VMEM((8, hd), F32),
            dma((8,)),
            dma((2, heads)),
            dma((heads,)),
        ]
        + [dma((z,))] * 4
        + [dma((heads, z))] * 6
        + [dma((e,))] * 4
        + [dma((z,))] * 4
        + [dma((e,))] * 2
        + [dma((f,))] * 2
        + [pltpu.SemaphoreType.REGULAR((n_sp,)), pltpu.SemaphoreType.REGULAR],
        compiler_params=pltpu.CompilerParams(
            collective_id=0, has_side_effects=True, vmem_limit_bytes=40 << 20
        ),
    )(
        *(
            pltpu.with_memory_space_constraint(operand, pltpu.HBM)
            for operand in (
                qkv,
                cotangent[0],
                text_kv,
                routes.reshape(1, text_rows),
                q_gain.reshape(1, hd),
                k_gain.reshape(1, hd),
                text_gain.reshape(1, hd),
            )
        )
    )
    results = (out_img, out_txt, out_gain)
    out_img, out_txt, out_gain = pl.pallas_call(
        write_out,
        out_shape=tuple(jax.ShapeDtypeStruct(r.shape, r.dtype) for r in results),
        in_specs=[vmem_spec] * 3,
        out_specs=(hbm_spec,) * 3,
        scratch_shapes=[dma((14,))],
    )(*(pltpu.with_memory_space_constraint(result, pltpu.VMEM) for result in results))
    return out_img.transpose(1, 0, 2)[None], out_txt, out_gain


def solution(mesh):
    sizes = tuple(mesh.shape[axis] for axis in ("fsdp", "sp", "enc"))
    placed = (
        P(("fsdp", "enc"), "sp", None, None),
        P(("fsdp", "enc"), "sp", None),
        P(("fsdp", "sp", "enc"), None, None),
        P(("fsdp", "sp", "enc"), None),
        P(),
        P(),
        P(),
    )
    return jax.shard_map(
        functools.partial(on_device, sizes),
        mesh=mesh,
        in_specs=placed,
        out_specs=(P(("fsdp", "enc"), "sp", None, None), P(("fsdp", "sp", "enc"), None, None), P()),
        check_vma=False,
    )
```

```python
import functools
import math

import jax
import jax.numpy as jnp
from jax import lax
from jax.experimental import pallas as pl
from jax.experimental.pallas import tpu as pltpu
from jax.sharding import PartitionSpec as P

EPSILON = 1e-06
CAP = 2
F32 = jnp.float32
BF16 = jnp.bfloat16
MESH = pl.DeviceIdType.MESH


def dot(a, b):
    return jnp.dot(a, b, preferred_element_type=F32)


def dot_nt(a, b):
    return lax.dot_general(a, b, (((1,), (1,)), ((), ())), preferred_element_type=F32)


def kernel(
    sizes,
    qkv,
    cot,
    txt,
    routes_hbm,
    q_gain_hbm,
    k_gain_hbm,
    t_gain_hbm,
    out_img,
    out_txt,
    out_gain,
    rows_in,
    grads_in,
    sends,
    routes_in,
    gains,
    text_in,
    slots,
    text_keys,
    text_sends,
    slots_back,
    text_back,
    gain_own,
    gain_z,
    gain_e,
    gain_f,
    place_t,
    qn_t,
    unit_t,
    factor_t,
    g_t,
    keys,
    keys_t,
    values,
    values_t,
    weights,
    packs,
    dk_sum,
    dv_sum,
    q_term,
    kt_term,
    own_sem,
    own_head,
    own_back,
    sg_send,
    sg_recv,
    tx_send,
    tx_recv,
    fw_send,
    fw_recv,
    ct_send,
    ct_recv,
    bk_send,
    bk_recv,
    en_send,
    en_recv,
    eb_send,
    eb_recv,
    tb_send,
    tb_recv,
    gz_send,
    gz_recv,
    ge_send,
    ge_recv,
    gf_send,
    gf_recv,
    above,
    line,
):
    n_fs, n_sp, n_en = sizes
    fs, sp, en = lax.axis_index("fsdp"), lax.axis_index("sp"), lax.axis_index("enc")
    rows, width = cot.shape
    text_rows = txt.shape[0]
    hd = gains.shape[2]
    q_gain, k_gain, t_gain = gains.at[0], gains.at[1], gains.at[2]
    local = width // n_sp
    heads = local // hd
    seq = rows * n_sp
    per_enc = CAP * n_sp
    n_slots = per_enc * n_en
    n_text = text_rows * n_sp
    scale = hd ** (-0.5)
    z_steps = sorted(range(1, n_sp), key=lambda d: min(d, n_sp - d))
    e_steps = list(range(1, n_en))
    f_steps = list(range(1, n_fs))

    def aligned(index, size):
        return pl.ds(pl.multiple_of(index * size, size), size)

    def on(axis, me, step, size):
        return {axis: lax.rem(me + step, size)}, lax.rem(me + step, size)

    layer = [("enc", en, step, n_en) for step in e_steps] + [("fsdp", fs, step, n_fs) for step in f_steps]
    barrier = pltpu.get_barrier_semaphore()

    def greet(sem, axis, me, step, size):
        pl.semaphore_signal(sem, inc=1, device_id=on(axis, me, step, size)[0], device_id_type=MESH)

    for step in range(1, n_sp):

        @pl.when(sp + step < n_sp)
        def _():
            greet(barrier, "sp", sp, step, n_sp)

    @pl.when(sp == 0)
    def _():
        for peer in layer:
            greet(barrier, *peer)

    def remote(src, dst, send, recv, device):
        return pltpu.make_async_remote_copy(
            src_ref=src, dst_ref=dst, send_sem=send, recv_sem=recv, device_id=device, device_id_type=MESH
        )

    def copy_routes(i):
        device, _ = on("sp", sp, z_steps[i], n_sp)
        return remote(routes_hbm, routes_in.at[sp], sg_send.at[i], sg_recv.at[i], device)

    def copy_text(i):
        device, peer = on("sp", sp, z_steps[i], n_sp)
        return remote(
            txt.at[:, :, aligned(peer, local)],
            text_in.at[aligned(sp, text_rows)],
            tx_send.at[i],
            tx_recv.at[i],
            device,
        )

    def copy_rows(h, i):
        device, peer = on("sp", sp, z_steps[i], n_sp)
        return remote(
            qkv.at[:, :, aligned(peer * heads + h, hd)],
            rows_in.at[h, :, aligned(sp, rows), :],
            fw_send.at[h, i],
            fw_recv.at[h, i],
            device,
        )

    def copy_cot(h, i):
        device, peer = on("sp", sp, z_steps[i], n_sp)
        return remote(
            cot.at[:, aligned(peer * heads + h, hd)],
            grads_in.at[h, aligned(sp, rows), :],
            ct_send.at[h, i],
            ct_recv.at[h, i],
            device,
        )

    def copy_back(h, i):
        device, peer = on("sp", sp, z_steps[i], n_sp)
        return remote(
            sends.at[h, :, aligned(peer, rows), :],
            out_img.at[:, :, aligned(sp * heads + h, hd)],
            bk_send.at[h, i],
            bk_recv.at[h, i],
            device,
        )

    def copy_slots(i):
        device, peer = on("enc", en, e_steps[i], n_en)
        return remote(
            slots.at[aligned(peer, per_enc)],
            text_keys.at[aligned(en, per_enc)],
            en_send.at[i],
            en_recv.at[i],
            device,
        )

    def copy_slots_back(i):
        device, peer = on("enc", en, e_steps[i], n_en)
        return remote(
            text_sends.at[aligned(peer, per_enc)],
            slots_back.at[aligned(en, per_enc)],
            eb_send.at[i],
            eb_recv.at[i],
            device,
        )

    def copy_text_back(i):
        device, peer = on("sp", sp, z_steps[i], n_sp)
        return remote(
            text_back.at[aligned(peer, text_rows)],
            out_txt.at[:, :, aligned(sp, local)],
            tb_send.at[i],
            tb_recv.at[i],
            device,
        )

    def copy_gain(i, level):
        axis, me, steps, size, own, dst, send, recv = (
            ("sp", sp, z_steps, n_sp, gain_own.at[0], gain_z, gz_send, gz_recv),
            ("enc", en, e_steps, n_en, gain_own.at[1], gain_e, ge_send, ge_recv),
            ("fsdp", fs, f_steps, n_fs, gain_own.at[2], gain_f, gf_send, gf_recv),
        )[level]
        device, _ = on(axis, me, steps[i], size)
        return remote(own, dst.at[me], send.at[i], recv.at[i], device)

    fetches = [pltpu.make_async_copy(routes_hbm, routes_in.at[sp], own_sem.at[0])] + [
        pltpu.make_async_copy(src, gains.at[n], own_sem.at[5 + n])
        for n, src in enumerate((q_gain_hbm, k_gain_hbm, t_gain_hbm))
    ]
    own_text = pltpu.make_async_copy(
        txt.at[:, :, aligned(sp, local)], text_in.at[aligned(sp, text_rows)], own_sem.at[1]
    )
    own_slots = pltpu.make_async_copy(
        slots.at[aligned(en, per_enc)], text_keys.at[aligned(en, per_enc)], own_sem.at[2]
    )
    own_slots_back = pltpu.make_async_copy(
        text_sends.at[aligned(en, per_enc)], slots_back.at[aligned(en, per_enc)], own_sem.at[3]
    )
    own_text_back = pltpu.make_async_copy(
        text_back.at[aligned(sp, text_rows)], out_txt.at[:, :, aligned(sp, local)], own_sem.at[4]
    )

    def own_rows(h):
        return pltpu.make_async_copy(
            qkv.at[:, :, aligned(sp * heads + h, hd)], rows_in.at[h, :, aligned(sp, rows), :], own_head.at[0, h]
        )

    def own_cot(h):
        return pltpu.make_async_copy(
            cot.at[:, aligned(sp * heads + h, hd)], grads_in.at[h, aligned(sp, rows), :], own_head.at[1, h]
        )

    def own_image_back(h):
        return pltpu.make_async_copy(
            sends.at[h, :, aligned(sp, rows), :], out_img.at[:, :, aligned(sp * heads + h, hd)], own_back.at[h]
        )

    pl.semaphore_wait(barrier, jnp.where(sp == 0, len(layer), sp))

    for step in range(1, n_sp):

        @pl.when(sp + step >= n_sp)
        def _():
            greet(above.at[n_sp - step], "sp", sp, step, n_sp)

    for fetch in fetches:
        fetch.start()
    own_text.start()
    for h in range(heads):
        own_rows(h).start()
        own_cot(h).start()

    def text_sends_to(step):
        i = z_steps.index(step)
        copy_routes(i).start()
        copy_text(i).start()

    def head_sends_to(step):
        i = z_steps.index(step)
        copy_rows(0, i).start()
        copy_cot(0, i).start()

    for step in z_steps:

        @pl.when(sp + step >= n_sp)
        def _():
            text_sends_to(step)

    for step in range(1, n_sp - 1):

        @pl.when(sp + step < n_sp - 1)
        def _():
            pl.semaphore_wait(above.at[step], 1)
            text_sends_to(step)

    for step in z_steps:

        @pl.when(sp + step != n_sp - 1)
        def _():
            head_sends_to(step)

    for step in range(1, n_sp):

        @pl.when(sp + step == n_sp - 1)
        def _():
            pl.semaphore_wait(above.at[step], 1)
            text_sends_to(step)
            head_sends_to(step)


    for h in range(1, heads):
        for i in range(len(z_steps)):
            copy_rows(h, i).start()
            copy_cot(h, i).start()

    @pl.when(sp == 0)
    def _():
        for peer in layer:
            greet(line, *peer)
        pl.semaphore_wait(line, len(layer))
        for step in range(1, n_sp):
            greet(line, "sp", sp, step, n_sp)

    @pl.when(sp > 0)
    def _():
        pl.semaphore_wait(line, 1)

    own_text.wait()
    for fetch in fetches:
        fetch.wait()
    for i in range(len(z_steps)):
        copy_routes(i).wait()
        copy_text(i).wait()
    row_at = lax.broadcasted_iota(jnp.int32, (text_rows, text_rows), 0)
    col_at = lax.broadcasted_iota(jnp.int32, (text_rows, text_rows), 1)
    slot_at = lax.broadcasted_iota(jnp.int32, (text_rows, n_slots), 1).astype(F32)
    placed_parts = []
    for shard in range(n_sp):
        dest_lane = jnp.broadcast_to(routes_in[shard].astype(F32), (text_rows, text_rows))
        dest_col = jnp.sum(jnp.where(row_at == col_at, dest_lane, 0.0), axis=1, keepdims=True)
        same = jnp.where((dest_col == dest_lane) & (col_at < row_at), 1.0, 0.0)
        rank = jnp.sum(same, axis=1, keepdims=True)
        slot = dest_col * per_enc + (shard * CAP) + rank
        placed_parts.append(jnp.where(slot == slot_at, 1.0, 0.0))
    placed_t = jnp.concatenate(placed_parts, axis=0)
    place_t[...] = placed_t.astype(BF16)
    placed = placed_t.T
    arrived = text_in[...].astype(F32)
    for part in range(2):
        slots[:, part * local : (part + 1) * local] = dot(
            placed.astype(BF16), arrived[:, part, :].astype(BF16)
        ).astype(BF16)
    live_col = jnp.sum(placed, axis=1, keepdims=True)
    slots[:, 2 * local :] = jnp.broadcast_to(live_col, (n_slots, hd)).astype(BF16)
    own_slots.start()
    for i in range(len(e_steps)):
        copy_slots(i).start()
    own_slots.wait()
    for i in range(len(e_steps)):
        copy_slots(i).wait()

    chunk = 256
    q_chunk = weights.shape[1]
    n_image = seq // chunk
    key_parts = [(c * chunk, chunk, False) for c in range(n_image)] + [(seq, n_slots, True)]
    gain_col = jnp.broadcast_to(q_gain[...], (hd, hd)).T
    q_gain_t = jnp.concatenate([gain_col] * (q_chunk // hd), axis=1)

    def norm_rows(raw, gain):
        factor = lax.rsqrt(jnp.mean(raw * raw, axis=-1, keepdims=True) + EPSILON)
        unit = raw * factor
        return unit * gain, unit, factor

    def norm_rows_back(grad, unit, factor, gain):
        scaled = grad * gain
        inner = jnp.mean(scaled * unit, axis=-1, keepdims=True)
        return factor * (scaled - unit * inner)

    def one_head(h, carry):
        own_rows(h).wait()
        own_cot(h).wait()
        for i in range(len(z_steps)):
            copy_rows(h, i).wait_recv()
            copy_cot(h, i).wait_recv()

        def prepare(c, carry):
            at = aligned(c, chunk)
            raw_t = rows_in[h, 0, at, :].astype(F32).T
            factor = lax.rsqrt(jnp.mean(raw_t * raw_t, axis=0, keepdims=True) + EPSILON)
            unit = raw_t * factor
            unit_t[:, at] = unit
            factor_t[:, at] = factor
            qn_t[:, at] = (unit * q_gain_t[:, :chunk]).astype(BF16)
            g_t[:, at] = grads_in[h, at, :].astype(F32).T
            normed = norm_rows(rows_in[h, 1, at, :].astype(F32), k_gain[...])[0]
            keys[at, :] = normed.astype(BF16)
            keys_t[:, at] = normed.T.astype(BF16)
            value = rows_in[h, 2, at, :]
            values[at, :] = value
            values_t[:, at] = value.astype(F32).T.astype(BF16)
            return carry

        lax.fori_loop(0, n_image, prepare, 0)
        text_at = pl.ds(seq, n_slots)
        normed = norm_rows(text_keys[:, aligned(h, hd)].astype(F32), t_gain[...])[0]
        keys[text_at, :] = normed.astype(BF16)
        keys_t[:, text_at] = normed.T.astype(BF16)
        value = text_keys[:, aligned(heads + h, hd)]
        values[text_at, :] = value
        values_t[:, text_at] = value.astype(F32).T.astype(BF16)
        dk_sum[...] = jnp.zeros_like(dk_sum)
        dv_sum[...] = jnp.zeros_like(dv_sum)

        def queries(j, carry):
            at = aligned(j, q_chunk)
            qn = qn_t[:, at]
            total = jnp.zeros((1, q_chunk), F32)
            numer = jnp.zeros((hd, q_chunk), F32)
            for first, count, is_text in key_parts:
                part = pl.ds(first, count)
                weight = jnp.exp2(dot(keys[part, :], qn) * (scale * math.log2(math.e)))
                if is_text:
                    live = text_keys[:, 2 * local :].astype(F32)
                    weight = weight * jnp.concatenate([live] * (q_chunk // hd), axis=1)
                total += jnp.sum(weight, axis=0, keepdims=True)
                packed = weight.astype(BF16)
                weights[part, :] = weight
                packs[part, :] = packed
                numer += dot(values_t[:, part], packed)
            inverse = 1.0 / total
            scaled_wide = g_t[:, at] * inverse
            scaled = scaled_wide.astype(BF16)
            grad_total = -jnp.sum(scaled_wide * (numer * inverse), axis=0, keepdims=True)
            dq = jnp.zeros((hd, q_chunk), F32)
            for first, count, _ in key_parts:
                part = pl.ds(first, count)
                back = dot(values[part, :], scaled)
                tangent = ((back + grad_total) * weights[part, :] * scale).astype(BF16)
                dq += dot(keys_t[:, part], tangent)
                dk_sum[part, :] += dot_nt(tangent, qn)
                dv_sum[part, :] += dot_nt(packs[part, :], scaled)
            unit = unit_t[:, at]
            q_term[...] += dq * unit
            spread = dq * q_gain_t
            inner = jnp.mean(spread * unit, axis=0, keepdims=True)
            dx = factor_t[:, at] * (spread - unit * inner)
            sends[h, 0, at, :] = dx.T.astype(BF16)
            return carry

        lax.fori_loop(0, seq // q_chunk, queries, 0)

        def finish(c, carry):
            at = aligned(c, chunk)
            dk = dk_sum[at, :]
            _, unit, factor = norm_rows(rows_in[h, 1, at, :].astype(F32), k_gain[...])
            kt_term[0:1, :] += jnp.sum(dk * unit, axis=0, keepdims=True)
            sends[h, 1, at, :] = norm_rows_back(dk, unit, factor, k_gain[...]).astype(BF16)
            sends[h, 2, at, :] = dv_sum[at, :].astype(BF16)
            return carry

        lax.fori_loop(0, n_image, finish, 0)
        dk = dk_sum[text_at, :]
        _, unit, factor = norm_rows(text_keys[:, aligned(h, hd)].astype(F32), t_gain[...])
        kt_term[1:2, :] += jnp.sum(dk * unit, axis=0, keepdims=True)
        text_sends[:, aligned(h, hd)] = norm_rows_back(dk, unit, factor, t_gain[...]).astype(BF16)
        text_sends[:, aligned(heads + h, hd)] = dv_sum[text_at, :].astype(BF16)

        @pl.when(h == heads - 1)
        def _():
            gain_own[0, :, 0:hd] = jnp.sum(q_term[...].T, axis=0, keepdims=True)
            gain_own[0, :, hd : 2 * hd] = kt_term[0:1, :]
            gain_own[0, :, 2 * hd : 3 * hd] = kt_term[1:2, :]
            gain_z[sp] = gain_own[0]
            for i in range(len(z_steps)):
                copy_gain(i, 0).start()
            own_slots_back.start()
            for i in range(len(e_steps)):
                copy_slots_back(i).start()

        for i in (0, 1, 6, 2, 3, 4, 5):
            copy_back(h, i).start()
        own_image_back(h).start()
        return carry

    q_term[...] = jnp.zeros_like(q_term)
    kt_term[...] = jnp.zeros_like(kt_term)
    lax.fori_loop(0, heads, one_head, 0)

    for i in range(len(z_steps)):
        copy_gain(i, 0).wait()
    gain_own[1] = jnp.sum(gain_z[...], axis=0)
    gain_e[en] = gain_own[1]
    for i in range(len(e_steps)):
        copy_gain(i, 1).start()
    own_slots_back.wait()
    for i in range(len(e_steps)):
        copy_slots_back(i).wait()
    mine = [dot(place_t[...], slots_back[:, part * local : (part + 1) * local]) for part in range(2)]
    text_back[...] = jnp.stack(mine, axis=1).astype(BF16)
    own_text_back.start()
    for i in range(len(z_steps)):
        copy_text_back(i).start()
    for i in range(len(e_steps)):
        copy_gain(i, 1).wait()
    gain_own[2] = jnp.sum(gain_e[...], axis=0)
    gain_f[fs] = gain_own[2]
    for i in range(len(f_steps)):
        copy_gain(i, 2).start()
    for i in range(len(f_steps)):
        copy_gain(i, 2).wait()
    sample_count = n_fs * n_en
    scale_total = float(sample_count * seq * heads * n_sp) ** (-0.5)
    total_gain = jnp.sum(gain_f[...], axis=0) * scale_total
    for n in range(3):
        out_gain[n : n + 1, :] = total_gain[:, n * hd : (n + 1) * hd]

    for h in range(heads):
        for i in range(len(z_steps)):
            copy_rows(h, i).wait_send()
            copy_cot(h, i).wait_send()
            copy_back(h, i).wait()
        own_image_back(h).wait()
    own_text_back.wait()
    for i in range(len(z_steps)):
        copy_text_back(i).wait()


def write_out(img, txt, gain, out_img, out_txt, out_gain, sems):
    pieces = 4
    rows = img.shape[1] // pieces
    pairs = [
        (img.at[t, p * rows : (p + 1) * rows], out_img.at[t, p * rows : (p + 1) * rows])
        for t in range(3)
        for p in range(pieces)
    ] + [(txt, out_txt), (gain, out_gain)]
    copies = [pltpu.make_async_copy(src, dst, sems.at[n]) for n, (src, dst) in enumerate(pairs)]
    for copy in copies:
        copy.start()
    for copy in copies:
        copy.wait()


def on_device(sizes, image_qkv, cotangent, text_kv, routes, q_gain, k_gain, text_gain):
    n_fs, n_sp, n_en = sizes
    _, rows, _, width = image_qkv.shape
    text_rows = text_kv.shape[0]
    hd = q_gain.shape[0]
    local = width // n_sp
    heads = local // hd
    seq = rows * n_sp
    n_slots = CAP * n_sp * n_en
    n_text = text_rows * n_sp
    n_keys = seq + n_slots
    q_chunk = 256
    qkv = image_qkv[0].transpose(1, 0, 2)
    dma = pltpu.SemaphoreType.DMA
    z, e, f = n_sp - 1, n_en - 1, n_fs - 1
    any_spec = pl.BlockSpec(memory_space=pl.ANY)
    hbm_spec = pl.BlockSpec(memory_space=pltpu.HBM)
    vmem_spec = pl.BlockSpec(memory_space=pltpu.VMEM)
    out_img, out_txt, out_gain = pl.pallas_call(
        functools.partial(kernel, sizes),
        out_shape=(
            pltpu.VMEM((3, rows, width), BF16),
            pltpu.VMEM((text_rows, 2, width), BF16),
            pltpu.VMEM((3, hd), F32),
        ),
        in_specs=[hbm_spec] * 7,
        out_specs=(any_spec, any_spec, vmem_spec),
        scratch_shapes=[
            pltpu.VMEM((heads, 3, seq, hd), BF16),
            pltpu.VMEM((heads, seq, hd), BF16),
            pltpu.VMEM((heads, 3, seq, hd), BF16),
            pltpu.VMEM((n_sp, 1, text_rows), jnp.int32),
            pltpu.VMEM((3, 1, hd), F32),
            pltpu.VMEM((n_text, 2, local), BF16),
            pltpu.VMEM((n_slots, 2 * local + hd), BF16),
            pltpu.VMEM((n_slots, 2 * local + hd), BF16),
            pltpu.VMEM((n_slots, 2 * local), BF16),
            pltpu.VMEM((n_slots, 2 * local), BF16),
            pltpu.VMEM((n_text, 2, local), BF16),
            pltpu.VMEM((3, 1, 3 * hd), F32),
            pltpu.VMEM((n_sp, 1, 3 * hd), F32),
            pltpu.VMEM((n_en, 1, 3 * hd), F32),
            pltpu.VMEM((n_fs, 1, 3 * hd), F32),
            pltpu.VMEM((n_text, n_slots), BF16),
            pltpu.VMEM((hd, seq), BF16),
            pltpu.VMEM((hd, seq), F32),
            pltpu.VMEM((1, seq), F32),
            pltpu.VMEM((hd, seq), F32),
            pltpu.VMEM((n_keys, hd), BF16),
            pltpu.VMEM((hd, n_keys), BF16),
            pltpu.VMEM((n_keys, hd), BF16),
            pltpu.VMEM((hd, n_keys), BF16),
            pltpu.VMEM((n_keys, q_chunk), F32),
            pltpu.VMEM((n_keys, q_chunk), BF16),
            pltpu.VMEM((n_keys, hd), F32),
            pltpu.VMEM((n_keys, hd), F32),
            pltpu.VMEM((hd, q_chunk), F32),
            pltpu.VMEM((8, hd), F32),
            dma((8,)),
            dma((2, heads)),
            dma((heads,)),
        ]
        + [dma((z,))] * 4
        + [dma((heads, z))] * 6
        + [dma((e,))] * 4
        + [dma((z,))] * 4
        + [dma((e,))] * 2
        + [dma((f,))] * 2
        + [pltpu.SemaphoreType.REGULAR((n_sp,)), pltpu.SemaphoreType.REGULAR],
        compiler_params=pltpu.CompilerParams(
            collective_id=0, has_side_effects=True, vmem_limit_bytes=40 << 20
        ),
    )(
        *(
            pltpu.with_memory_space_constraint(operand, pltpu.HBM)
            for operand in (
                qkv,
                cotangent[0],
                text_kv,
                routes.reshape(1, text_rows),
                q_gain.reshape(1, hd),
                k_gain.reshape(1, hd),
                text_gain.reshape(1, hd),
            )
        )
    )
    results = (out_img, out_txt, out_gain)
    out_img, out_txt, out_gain = pl.pallas_call(
        write_out,
        out_shape=tuple(jax.ShapeDtypeStruct(r.shape, r.dtype) for r in results),
        in_specs=[vmem_spec] * 3,
        out_specs=(hbm_spec,) * 3,
        scratch_shapes=[dma((14,))],
    )(*(pltpu.with_memory_space_constraint(result, pltpu.VMEM) for result in results))
    return out_img.transpose(1, 0, 2)[None], out_txt, out_gain


def solution(mesh):
    sizes = tuple(mesh.shape[axis] for axis in ("fsdp", "sp", "enc"))
    placed = (
        P(("fsdp", "enc"), "sp", None, None),
        P(("fsdp", "enc"), "sp", None),
        P(("fsdp", "sp", "enc"), None, None),
        P(("fsdp", "sp", "enc"), None),
        P(),
        P(),
        P(),
    )
    return jax.shard_map(
        functools.partial(on_device, sizes),
        mesh=mesh,
        in_specs=placed,
        out_specs=(P(("fsdp", "enc"), "sp", None, None), P(("fsdp", "sp", "enc"), None, None), P()),
        check_vma=False,
    )
```

```python
import functools
import math

import jax
import jax.numpy as jnp
from jax import lax
from jax.experimental import pallas as pl
from jax.experimental.pallas import tpu as pltpu
from jax.sharding import PartitionSpec as P

EPSILON = 1e-06
CAP = 2
F32 = jnp.float32
BF16 = jnp.bfloat16
MESH = pl.DeviceIdType.MESH


def dot(a, b):
    return jnp.dot(a, b, preferred_element_type=F32)


def dot_nt(a, b):
    return lax.dot_general(a, b, (((1,), (1,)), ((), ())), preferred_element_type=F32)


def kernel(
    sizes,
    qkv,
    cot,
    txt,
    routes_hbm,
    q_gain_hbm,
    k_gain_hbm,
    t_gain_hbm,
    out_img,
    out_txt,
    out_gain,
    rows_in,
    grads_in,
    sends,
    routes_in,
    gains,
    text_in,
    slots,
    text_keys,
    text_sends,
    slots_back,
    text_back,
    gain_own,
    gain_z,
    gain_e,
    gain_f,
    place_t,
    qn_t,
    unit_t,
    factor_t,
    g_t,
    keys,
    keys_t,
    values,
    values_t,
    weights,
    packs,
    dk_sum,
    dv_sum,
    q_term,
    kt_term,
    own_sem,
    own_head,
    own_back,
    sg_send,
    sg_recv,
    tx_send,
    tx_recv,
    fw_send,
    fw_recv,
    ct_send,
    ct_recv,
    bk_send,
    bk_recv,
    en_send,
    en_recv,
    eb_send,
    eb_recv,
    tb_send,
    tb_recv,
    gz_send,
    gz_recv,
    ge_send,
    ge_recv,
    gf_send,
    gf_recv,
    above,
    line,
):
    n_fs, n_sp, n_en = sizes
    fs, sp, en = lax.axis_index("fsdp"), lax.axis_index("sp"), lax.axis_index("enc")
    rows, width = cot.shape
    text_rows = txt.shape[0]
    hd = gains.shape[2]
    q_gain, k_gain, t_gain = gains.at[0], gains.at[1], gains.at[2]
    local = width // n_sp
    heads = local // hd
    seq = rows * n_sp
    per_enc = CAP * n_sp
    n_slots = per_enc * n_en
    n_text = text_rows * n_sp
    scale = hd ** (-0.5)
    z_steps = sorted(range(1, n_sp), key=lambda d: min(d, n_sp - d))
    e_steps = list(range(1, n_en))
    f_steps = list(range(1, n_fs))

    def aligned(index, size):
        return pl.ds(pl.multiple_of(index * size, size), size)

    def on(axis, me, step, size):
        return {axis: lax.rem(me + step, size)}, lax.rem(me + step, size)

    layer = [("enc", en, step, n_en) for step in e_steps] + [("fsdp", fs, step, n_fs) for step in f_steps]
    barrier = pltpu.get_barrier_semaphore()

    def greet(sem, axis, me, step, size):
        pl.semaphore_signal(sem, inc=1, device_id=on(axis, me, step, size)[0], device_id_type=MESH)

    for step in range(1, n_sp):

        @pl.when(sp + step < n_sp)
        def _():
            greet(barrier, "sp", sp, step, n_sp)

    @pl.when(sp == 0)
    def _():
        for peer in layer:
            greet(barrier, *peer)

    def remote(src, dst, send, recv, device):
        return pltpu.make_async_remote_copy(
            src_ref=src, dst_ref=dst, send_sem=send, recv_sem=recv, device_id=device, device_id_type=MESH
        )

    def copy_routes(i):
        device, _ = on("sp", sp, z_steps[i], n_sp)
        return remote(routes_hbm, routes_in.at[sp], sg_send.at[i], sg_recv.at[i], device)

    def copy_text(i):
        device, peer = on("sp", sp, z_steps[i], n_sp)
        return remote(
            txt.at[:, :, aligned(peer, local)],
            text_in.at[aligned(sp, text_rows)],
            tx_send.at[i],
            tx_recv.at[i],
            device,
        )

    def copy_rows(h, i):
        device, peer = on("sp", sp, z_steps[i], n_sp)
        return remote(
            qkv.at[:, :, aligned(peer * heads + h, hd)],
            rows_in.at[h, :, aligned(sp, rows), :],
            fw_send.at[h, i],
            fw_recv.at[h, i],
            device,
        )

    def copy_cot(h, i):
        device, peer = on("sp", sp, z_steps[i], n_sp)
        return remote(
            cot.at[:, aligned(peer * heads + h, hd)],
            grads_in.at[h, aligned(sp, rows), :],
            ct_send.at[h, i],
            ct_recv.at[h, i],
            device,
        )

    def copy_back(h, i):
        device, peer = on("sp", sp, z_steps[i], n_sp)
        return remote(
            sends.at[h, :, aligned(peer, rows), :],
            out_img.at[:, :, aligned(sp * heads + h, hd)],
            bk_send.at[h, i],
            bk_recv.at[h, i],
            device,
        )

    def copy_slots(i):
        device, peer = on("enc", en, e_steps[i], n_en)
        return remote(
            slots.at[aligned(peer, per_enc)],
            text_keys.at[aligned(en, per_enc)],
            en_send.at[i],
            en_recv.at[i],
            device,
        )

    def copy_slots_back(i):
        device, peer = on("enc", en, e_steps[i], n_en)
        return remote(
            text_sends.at[aligned(peer, per_enc)],
            slots_back.at[aligned(en, per_enc)],
            eb_send.at[i],
            eb_recv.at[i],
            device,
        )

    def copy_text_back(i):
        device, peer = on("sp", sp, z_steps[i], n_sp)
        return remote(
            text_back.at[aligned(peer, text_rows)],
            out_txt.at[:, :, aligned(sp, local)],
            tb_send.at[i],
            tb_recv.at[i],
            device,
        )

    def copy_gain(i, level):
        axis, me, steps, size, own, dst, send, recv = (
            ("sp", sp, z_steps, n_sp, gain_own.at[0], gain_z, gz_send, gz_recv),
            ("enc", en, e_steps, n_en, gain_own.at[1], gain_e, ge_send, ge_recv),
            ("fsdp", fs, f_steps, n_fs, gain_own.at[2], gain_f, gf_send, gf_recv),
        )[level]
        device, _ = on(axis, me, steps[i], size)
        return remote(own, dst.at[me], send.at[i], recv.at[i], device)

    fetches = [pltpu.make_async_copy(routes_hbm, routes_in.at[sp], own_sem.at[0])] + [
        pltpu.make_async_copy(src, gains.at[n], own_sem.at[5 + n])
        for n, src in enumerate((q_gain_hbm, k_gain_hbm, t_gain_hbm))
    ]
    own_text = pltpu.make_async_copy(
        txt.at[:, :, aligned(sp, local)], text_in.at[aligned(sp, text_rows)], own_sem.at[1]
    )
    own_slots = pltpu.make_async_copy(
        slots.at[aligned(en, per_enc)], text_keys.at[aligned(en, per_enc)], own_sem.at[2]
    )
    own_slots_back = pltpu.make_async_copy(
        text_sends.at[aligned(en, per_enc)], slots_back.at[aligned(en, per_enc)], own_sem.at[3]
    )
    own_text_back = pltpu.make_async_copy(
        text_back.at[aligned(sp, text_rows)], out_txt.at[:, :, aligned(sp, local)], own_sem.at[4]
    )

    def own_rows(h):
        return pltpu.make_async_copy(
            qkv.at[:, :, aligned(sp * heads + h, hd)], rows_in.at[h, :, aligned(sp, rows), :], own_head.at[0, h]
        )

    def own_cot(h):
        return pltpu.make_async_copy(
            cot.at[:, aligned(sp * heads + h, hd)], grads_in.at[h, aligned(sp, rows), :], own_head.at[1, h]
        )

    def own_image_back(h):
        return pltpu.make_async_copy(
            sends.at[h, :, aligned(sp, rows), :], out_img.at[:, :, aligned(sp * heads + h, hd)], own_back.at[h]
        )

    pl.semaphore_wait(barrier, jnp.where(sp == 0, len(layer), sp))

    for step in range(1, n_sp):

        @pl.when(sp + step >= n_sp)
        def _():
            greet(above.at[n_sp - step], "sp", sp, step, n_sp)

    for fetch in fetches:
        fetch.start()
    own_text.start()
    for h in range(heads):
        own_rows(h).start()
        own_cot(h).start()

    def text_sends_to(step):
        i = z_steps.index(step)
        copy_routes(i).start()
        copy_text(i).start()

    def head_sends_to(step):
        i = z_steps.index(step)
        copy_rows(0, i).start()
        copy_cot(0, i).start()

    for step in z_steps:

        @pl.when(sp + step >= n_sp)
        def _():
            text_sends_to(step)

    late = n_sp - 3

    for step in range(1, late):

        @pl.when(sp + step < late)
        def _():
            pl.semaphore_wait(above.at[step], 1)
            text_sends_to(step)

    for step in z_steps:

        @pl.when(jnp.logical_or(sp + step < late, sp + step >= n_sp))
        def _():
            head_sends_to(step)

    for step in range(1, n_sp):

        @pl.when(jnp.logical_and(sp + step >= late, sp + step < n_sp))
        def _():
            pl.semaphore_wait(above.at[step], 1)
            text_sends_to(step)
            head_sends_to(step)


    for h in range(1, heads):
        for i in range(len(z_steps)):
            copy_rows(h, i).start()
            copy_cot(h, i).start()

    @pl.when(sp == 0)
    def _():
        for peer in layer:
            greet(line, *peer)
        pl.semaphore_wait(line, len(layer))
        for step in range(1, n_sp):
            greet(line, "sp", sp, step, n_sp)

    @pl.when(sp > 0)
    def _():
        pl.semaphore_wait(line, 1)

    own_text.wait()
    for fetch in fetches:
        fetch.wait()
    for i in range(len(z_steps)):
        copy_routes(i).wait()
        copy_text(i).wait()
    row_at = lax.broadcasted_iota(jnp.int32, (text_rows, text_rows), 0)
    col_at = lax.broadcasted_iota(jnp.int32, (text_rows, text_rows), 1)
    slot_at = lax.broadcasted_iota(jnp.int32, (text_rows, n_slots), 1).astype(F32)
    placed_parts = []
    for shard in range(n_sp):
        dest_lane = jnp.broadcast_to(routes_in[shard].astype(F32), (text_rows, text_rows))
        dest_col = jnp.sum(jnp.where(row_at == col_at, dest_lane, 0.0), axis=1, keepdims=True)
        same = jnp.where((dest_col == dest_lane) & (col_at < row_at), 1.0, 0.0)
        rank = jnp.sum(same, axis=1, keepdims=True)
        slot = dest_col * per_enc + (shard * CAP) + rank
        placed_parts.append(jnp.where(slot == slot_at, 1.0, 0.0))
    placed_t = jnp.concatenate(placed_parts, axis=0)
    place_t[...] = placed_t.astype(BF16)
    placed = placed_t.T
    arrived = text_in[...].astype(F32)
    for part in range(2):
        slots[:, part * local : (part + 1) * local] = dot(
            placed.astype(BF16), arrived[:, part, :].astype(BF16)
        ).astype(BF16)
    live_col = jnp.sum(placed, axis=1, keepdims=True)
    slots[:, 2 * local :] = jnp.broadcast_to(live_col, (n_slots, hd)).astype(BF16)
    own_slots.start()
    for i in range(len(e_steps)):
        copy_slots(i).start()
    own_slots.wait()
    for i in range(len(e_steps)):
        copy_slots(i).wait()

    chunk = 256
    q_chunk = weights.shape[1]
    n_image = seq // chunk
    key_parts = [(c * chunk, chunk, False) for c in range(n_image)] + [(seq, n_slots, True)]
    gain_col = jnp.broadcast_to(q_gain[...], (hd, hd)).T
    q_gain_t = jnp.concatenate([gain_col] * (q_chunk // hd), axis=1)

    def norm_rows(raw, gain):
        factor = lax.rsqrt(jnp.mean(raw * raw, axis=-1, keepdims=True) + EPSILON)
        unit = raw * factor
        return unit * gain, unit, factor

    def norm_rows_back(grad, unit, factor, gain):
        scaled = grad * gain
        inner = jnp.mean(scaled * unit, axis=-1, keepdims=True)
        return factor * (scaled - unit * inner)

    def one_head(h, carry):
        own_rows(h).wait()
        own_cot(h).wait()
        for i in range(len(z_steps)):
            copy_rows(h, i).wait_recv()
            copy_cot(h, i).wait_recv()

        def prepare(c, carry):
            at = aligned(c, chunk)
            raw_t = rows_in[h, 0, at, :].astype(F32).T
            factor = lax.rsqrt(jnp.mean(raw_t * raw_t, axis=0, keepdims=True) + EPSILON)
            unit = raw_t * factor
            unit_t[:, at] = unit
            factor_t[:, at] = factor
            qn_t[:, at] = (unit * q_gain_t[:, :chunk]).astype(BF16)
            g_t[:, at] = grads_in[h, at, :].astype(F32).T
            normed = norm_rows(rows_in[h, 1, at, :].astype(F32), k_gain[...])[0]
            keys[at, :] = normed.astype(BF16)
            keys_t[:, at] = normed.T.astype(BF16)
            value = rows_in[h, 2, at, :]
            values[at, :] = value
            values_t[:, at] = value.astype(F32).T.astype(BF16)
            return carry

        lax.fori_loop(0, n_image, prepare, 0)
        text_at = pl.ds(seq, n_slots)
        normed = norm_rows(text_keys[:, aligned(h, hd)].astype(F32), t_gain[...])[0]
        keys[text_at, :] = normed.astype(BF16)
        keys_t[:, text_at] = normed.T.astype(BF16)
        value = text_keys[:, aligned(heads + h, hd)]
        values[text_at, :] = value
        values_t[:, text_at] = value.astype(F32).T.astype(BF16)
        dk_sum[...] = jnp.zeros_like(dk_sum)
        dv_sum[...] = jnp.zeros_like(dv_sum)

        def queries(j, carry):
            at = aligned(j, q_chunk)
            qn = qn_t[:, at]
            total = jnp.zeros((1, q_chunk), F32)
            numer = jnp.zeros((hd, q_chunk), F32)
            for first, count, is_text in key_parts:
                part = pl.ds(first, count)
                weight = jnp.exp2(dot(keys[part, :], qn) * (scale * math.log2(math.e)))
                if is_text:
                    live = text_keys[:, 2 * local :].astype(F32)
                    weight = weight * jnp.concatenate([live] * (q_chunk // hd), axis=1)
                total += jnp.sum(weight, axis=0, keepdims=True)
                packed = weight.astype(BF16)
                weights[part, :] = weight
                packs[part, :] = packed
                numer += dot(values_t[:, part], packed)
            inverse = 1.0 / total
            scaled_wide = g_t[:, at] * inverse
            scaled = scaled_wide.astype(BF16)
            grad_total = -jnp.sum(scaled_wide * (numer * inverse), axis=0, keepdims=True)
            dq = jnp.zeros((hd, q_chunk), F32)
            for first, count, _ in key_parts:
                part = pl.ds(first, count)
                back = dot(values[part, :], scaled)
                tangent = ((back + grad_total) * weights[part, :] * scale).astype(BF16)
                dq += dot(keys_t[:, part], tangent)
                dk_sum[part, :] += dot_nt(tangent, qn)
                dv_sum[part, :] += dot_nt(packs[part, :], scaled)
            unit = unit_t[:, at]
            q_term[...] += dq * unit
            spread = dq * q_gain_t
            inner = jnp.mean(spread * unit, axis=0, keepdims=True)
            dx = factor_t[:, at] * (spread - unit * inner)
            sends[h, 0, at, :] = dx.T.astype(BF16)
            return carry

        lax.fori_loop(0, seq // q_chunk, queries, 0)

        def finish(c, carry):
            at = aligned(c, chunk)
            dk = dk_sum[at, :]
            _, unit, factor = norm_rows(rows_in[h, 1, at, :].astype(F32), k_gain[...])
            kt_term[0:1, :] += jnp.sum(dk * unit, axis=0, keepdims=True)
            sends[h, 1, at, :] = norm_rows_back(dk, unit, factor, k_gain[...]).astype(BF16)
            sends[h, 2, at, :] = dv_sum[at, :].astype(BF16)
            return carry

        lax.fori_loop(0, n_image, finish, 0)
        dk = dk_sum[text_at, :]
        _, unit, factor = norm_rows(text_keys[:, aligned(h, hd)].astype(F32), t_gain[...])
        kt_term[1:2, :] += jnp.sum(dk * unit, axis=0, keepdims=True)
        text_sends[:, aligned(h, hd)] = norm_rows_back(dk, unit, factor, t_gain[...]).astype(BF16)
        text_sends[:, aligned(heads + h, hd)] = dv_sum[text_at, :].astype(BF16)

        @pl.when(h == heads - 1)
        def _():
            gain_own[0, :, 0:hd] = jnp.sum(q_term[...].T, axis=0, keepdims=True)
            gain_own[0, :, hd : 2 * hd] = kt_term[0:1, :]
            gain_own[0, :, 2 * hd : 3 * hd] = kt_term[1:2, :]
            gain_z[sp] = gain_own[0]
            for i in range(len(z_steps)):
                copy_gain(i, 0).start()
            own_slots_back.start()
            for i in range(len(e_steps)):
                copy_slots_back(i).start()

        for i in (0, 1, 6, 2, 3, 4, 5):
            copy_back(h, i).start()
        own_image_back(h).start()
        return carry

    q_term[...] = jnp.zeros_like(q_term)
    kt_term[...] = jnp.zeros_like(kt_term)
    lax.fori_loop(0, heads, one_head, 0)

    for i in range(len(z_steps)):
        copy_gain(i, 0).wait()
    gain_own[1] = jnp.sum(gain_z[...], axis=0)
    gain_e[en] = gain_own[1]
    for i in range(len(e_steps)):
        copy_gain(i, 1).start()
    own_slots_back.wait()
    for i in range(len(e_steps)):
        copy_slots_back(i).wait()
    mine = [dot(place_t[...], slots_back[:, part * local : (part + 1) * local]) for part in range(2)]
    text_back[...] = jnp.stack(mine, axis=1).astype(BF16)
    own_text_back.start()
    for i in range(len(z_steps)):
        copy_text_back(i).start()
    for i in range(len(e_steps)):
        copy_gain(i, 1).wait()
    gain_own[2] = jnp.sum(gain_e[...], axis=0)
    gain_f[fs] = gain_own[2]
    for i in range(len(f_steps)):
        copy_gain(i, 2).start()
    for i in range(len(f_steps)):
        copy_gain(i, 2).wait()
    sample_count = n_fs * n_en
    scale_total = float(sample_count * seq * heads * n_sp) ** (-0.5)
    total_gain = jnp.sum(gain_f[...], axis=0) * scale_total
    for n in range(3):
        out_gain[n : n + 1, :] = total_gain[:, n * hd : (n + 1) * hd]

    for h in range(heads):
        for i in range(len(z_steps)):
            copy_rows(h, i).wait_send()
            copy_cot(h, i).wait_send()
            copy_back(h, i).wait()
        own_image_back(h).wait()
    own_text_back.wait()
    for i in range(len(z_steps)):
        copy_text_back(i).wait()


def write_out(img, txt, gain, out_img, out_txt, out_gain, sems):
    pieces = 4
    rows = img.shape[1] // pieces
    pairs = [
        (img.at[t, p * rows : (p + 1) * rows], out_img.at[t, p * rows : (p + 1) * rows])
        for t in range(3)
        for p in range(pieces)
    ] + [(txt, out_txt), (gain, out_gain)]
    copies = [pltpu.make_async_copy(src, dst, sems.at[n]) for n, (src, dst) in enumerate(pairs)]
    for copy in copies:
        copy.start()
    for copy in copies:
        copy.wait()


def on_device(sizes, image_qkv, cotangent, text_kv, routes, q_gain, k_gain, text_gain):
    n_fs, n_sp, n_en = sizes
    _, rows, _, width = image_qkv.shape
    text_rows = text_kv.shape[0]
    hd = q_gain.shape[0]
    local = width // n_sp
    heads = local // hd
    seq = rows * n_sp
    n_slots = CAP * n_sp * n_en
    n_text = text_rows * n_sp
    n_keys = seq + n_slots
    q_chunk = 256
    qkv = image_qkv[0].transpose(1, 0, 2)
    dma = pltpu.SemaphoreType.DMA
    z, e, f = n_sp - 1, n_en - 1, n_fs - 1
    any_spec = pl.BlockSpec(memory_space=pl.ANY)
    hbm_spec = pl.BlockSpec(memory_space=pltpu.HBM)
    vmem_spec = pl.BlockSpec(memory_space=pltpu.VMEM)
    out_img, out_txt, out_gain = pl.pallas_call(
        functools.partial(kernel, sizes),
        out_shape=(
            pltpu.VMEM((3, rows, width), BF16),
            pltpu.VMEM((text_rows, 2, width), BF16),
            pltpu.VMEM((3, hd), F32),
        ),
        in_specs=[hbm_spec] * 7,
        out_specs=(any_spec, any_spec, vmem_spec),
        scratch_shapes=[
            pltpu.VMEM((heads, 3, seq, hd), BF16),
            pltpu.VMEM((heads, seq, hd), BF16),
            pltpu.VMEM((heads, 3, seq, hd), BF16),
            pltpu.VMEM((n_sp, 1, text_rows), jnp.int32),
            pltpu.VMEM((3, 1, hd), F32),
            pltpu.VMEM((n_text, 2, local), BF16),
            pltpu.VMEM((n_slots, 2 * local + hd), BF16),
            pltpu.VMEM((n_slots, 2 * local + hd), BF16),
            pltpu.VMEM((n_slots, 2 * local), BF16),
            pltpu.VMEM((n_slots, 2 * local), BF16),
            pltpu.VMEM((n_text, 2, local), BF16),
            pltpu.VMEM((3, 1, 3 * hd), F32),
            pltpu.VMEM((n_sp, 1, 3 * hd), F32),
            pltpu.VMEM((n_en, 1, 3 * hd), F32),
            pltpu.VMEM((n_fs, 1, 3 * hd), F32),
            pltpu.VMEM((n_text, n_slots), BF16),
            pltpu.VMEM((hd, seq), BF16),
            pltpu.VMEM((hd, seq), F32),
            pltpu.VMEM((1, seq), F32),
            pltpu.VMEM((hd, seq), F32),
            pltpu.VMEM((n_keys, hd), BF16),
            pltpu.VMEM((hd, n_keys), BF16),
            pltpu.VMEM((n_keys, hd), BF16),
            pltpu.VMEM((hd, n_keys), BF16),
            pltpu.VMEM((n_keys, q_chunk), F32),
            pltpu.VMEM((n_keys, q_chunk), BF16),
            pltpu.VMEM((n_keys, hd), F32),
            pltpu.VMEM((n_keys, hd), F32),
            pltpu.VMEM((hd, q_chunk), F32),
            pltpu.VMEM((8, hd), F32),
            dma((8,)),
            dma((2, heads)),
            dma((heads,)),
        ]
        + [dma((z,))] * 4
        + [dma((heads, z))] * 6
        + [dma((e,))] * 4
        + [dma((z,))] * 4
        + [dma((e,))] * 2
        + [dma((f,))] * 2
        + [pltpu.SemaphoreType.REGULAR((n_sp,)), pltpu.SemaphoreType.REGULAR],
        compiler_params=pltpu.CompilerParams(
            collective_id=0, has_side_effects=True, vmem_limit_bytes=40 << 20
        ),
    )(
        *(
            pltpu.with_memory_space_constraint(operand, pltpu.HBM)
            for operand in (
                qkv,
                cotangent[0],
                text_kv,
                routes.reshape(1, text_rows),
                q_gain.reshape(1, hd),
                k_gain.reshape(1, hd),
                text_gain.reshape(1, hd),
            )
        )
    )
    results = (out_img, out_txt, out_gain)
    out_img, out_txt, out_gain = pl.pallas_call(
        write_out,
        out_shape=tuple(jax.ShapeDtypeStruct(r.shape, r.dtype) for r in results),
        in_specs=[vmem_spec] * 3,
        out_specs=(hbm_spec,) * 3,
        scratch_shapes=[dma((14,))],
    )(*(pltpu.with_memory_space_constraint(result, pltpu.VMEM) for result in results))
    return out_img.transpose(1, 0, 2)[None], out_txt, out_gain


def solution(mesh):
    sizes = tuple(mesh.shape[axis] for axis in ("fsdp", "sp", "enc"))
    placed = (
        P(("fsdp", "enc"), "sp", None, None),
        P(("fsdp", "enc"), "sp", None),
        P(("fsdp", "sp", "enc"), None, None),
        P(("fsdp", "sp", "enc"), None),
        P(),
        P(),
        P(),
    )
    return jax.shard_map(
        functools.partial(on_device, sizes),
        mesh=mesh,
        in_specs=placed,
        out_specs=(P(("fsdp", "enc"), "sp", None, None), P(("fsdp", "sp", "enc"), None, None), P()),
        check_vma=False,
    )
```
